32 devices in a mesh: dp: 8 (over y, x, core), mp: 4 (over z).
Axes of the slice: x: 2, y: 2, z: 4, core: 2. Of those that a mesh axis runs over, the one named last changes fastest.
Arguments:
- hidden_in: bfloat16 [16384, 1024], P(('dp', 'mp')), may hold values from -6 to 6
- first_in: bfloat16 [16384, 1024], P(('dp', 'mp'))
- segment_ids: int32 [16384], P('dp'), may hold values from 0 to 23, as said below
- valid_tokens: int32 [16384], P('dp'), may hold values from 0 to 1, as said below
- w_query: bfloat16 [1024, 1024], P(None, 'mp'), may hold values from -0.1875 to 0.1875
- w_key: bfloat16 [1024, 1024], P(None, 'mp'), may hold values from -0.1875 to 0.1875
- w_value: bfloat16 [1024, 1024], P(None, 'mp'), may hold values from -0.1875 to 0.1875
- w_first_value: bfloat16 [1024, 1024], P(None, 'mp'), may hold values from -0.1875 to 0.1875
- w_out: bfloat16 [1024, 1024], P('mp'), may hold values from -1 to 1
- w_gate: bfloat16 [1024, 2816], P(None, 'mp'), may hold values from -0.1875 to 0.1875
- w_up: bfloat16 [1024, 2816], P(None, 'mp'), may hold values from -0.1875 to 0.1875
- w_down: bfloat16 [2816, 1024], P('mp'), may hold values from -0.109375 to 0.109375
- gain_attn: float32 [1024], replicated, may hold values from 0.5 to 1.5
- gain_mlp: float32 [1024], replicated, may hold values from 0.5 to 1.5
- out_cotangent: bfloat16 [16384, 1024], P('dp'), may hold values from -6 to 6
Outputs:
- block_out: bfloat16 [16384, 1024], P(('dp', 'mp'))
- grad_input: bfloat16 [16384, 1024], P(('dp', 'mp'))
- grad_query: float32 [1024, 1024], P(None, 'mp')
- grad_key: float32 [1024, 1024], P(None, 'mp')
- grad_value: float32 [1024, 1024], P(None, 'mp')
- grad_first_value: float32 [1024, 1024], P(None, 'mp')
- grad_out: float32 [1024, 1024], P('mp')
- grad_gate: float32 [1024, 2816], P(None, 'mp')
- grad_up: float32 [1024, 2816], P(None, 'mp')
- grad_down: float32 [2816, 1024], P('mp')
- grad_gain_attn: float32 [1024], replicated
- grad_gain_mlp: float32 [1024], replicated
- first_power: float32 [], replicated
- blend_power: float32 [], replicated
The draws below stay inside these ranges and needn't reach their ends.
Inputs may be any that keep to these rules, and one draw needn't show every extreme that they name: `segment_ids`: each packed sequence of 2048 tokens starts a new document, holds a short document, a long one and padding at its end; ids are distinct across sequences and never fall. `valid_tokens`: 0 exactly on the padding at the end of each sequence; padding has a segment id of its own.
All inputs are finite; a program needn't handle non-finite values.
Results may differ from the reference program's by a relative error of at most 0.022.
Values may be sent and summed in bfloat16 or wider, within the bound.
No kernel may reach another device: no remote copies, remote signals or barrier semaphores. Data moves between devices by JAX's collectives and lax.ppermute only.
A program may use at most 192 MiB of HBM per device.

```python
import math
import jax
import jax.numpy as jnp
from jax import lax

D = 1024
H = 16
HD = 64
FF = 2816
SEQ = 2048
TOKENS = 16384


def doc_layout(key):
    n_seqs = TOKENS // SEQ
    lead_key, tail_key = jax.random.split(key)
    lead = jax.random.randint(lead_key, (n_seqs, 1), 1, SEQ // 8 + 1)
    tail = jax.random.randint(tail_key, (n_seqs, 1), 1, SEQ // 16 + 1)
    place = jnp.arange(SEQ, dtype=jnp.int32)[None, :]
    piece = (place >= lead).astype(jnp.int32) + (place >= SEQ - tail).astype(jnp.int32)
    doc_ids = jnp.arange(n_seqs, dtype=jnp.int32)[:, None] * 3 + piece
    live_rows = (place < SEQ - tail).astype(jnp.int32)
    return (doc_ids.reshape(TOKENS), live_rows.reshape(TOKENS))


def draw_segment_ids(key, part):
    doc_ids, live_rows = doc_layout(key)
    return doc_ids


def draw_valid_tokens(key, part):
    doc_ids, live_rows = doc_layout(key)
    return live_rows


def draw_first_in(key, part):
    key = jax.random.fold_in(key, 7)
    rising = 0.6 + 0.6 * jnp.arange(TOKENS, dtype=jnp.float32)[:, None] / TOKENS
    base = jax.random.normal(key, (TOKENS, D), jnp.float32)
    return (base * rising).astype(jnp.bfloat16)


def steps_of(rng, dims, cuts, smallest, high):
    level = 1.0
    for axis_at, blocks in cuts:
        draws = jax.random.uniform(jax.random.fold_in(jax.random.fold_in(rng, 6), axis_at), (blocks,), jnp.float32, smallest / len(cuts), high / len(cuts))
        level = level * jnp.repeat(jnp.exp(draws), dims[axis_at] // blocks).reshape((-1,) + (1,) * (len(dims) - 1 - axis_at))
    return level


def bell_draw(stream_key, shape, scale, limit, shards=(), kind=jnp.bfloat16):
    gain = steps_of(stream_key, shape, shards, -0.22, 0.18) if shards else 1.0
    values = jax.random.normal(stream_key, shape, jnp.float32) * scale * gain
    return jnp.minimum(jnp.maximum(values, -limit), limit).astype(kind)


def setup_inputs(seed: int = 0) -> dict:
    key_list = jax.random.split(jax.random.key(seed), 16)
    return {
        "hidden_in": bell_draw(key_list[0], (TOKENS, D), 1.0, 6.0, ((0, 32),)),
        "first_in": draw_first_in(jax.random.fold_in(key_list[15], 71), 0),
        "segment_ids": draw_segment_ids(jax.random.fold_in(key_list[15], 71), 0),
        "valid_tokens": draw_valid_tokens(jax.random.fold_in(key_list[15], 71), 0),
        "w_query": bell_draw(key_list[4], (D, D), D ** -0.5, 0.1875, ((1, 4),)),
        "w_key": bell_draw(key_list[5], (D, D), D ** -0.5, 0.1875, ((1, 4),)),
        "w_value": bell_draw(key_list[6], (D, D), D ** -0.5, 0.1875, ((1, 4),)),
        "w_first_value": bell_draw(key_list[7], (D, D), D ** -0.5, 0.1875, ((1, 4),)),
        "w_out": bell_draw(key_list[8], (D, D), (D // 32) ** -0.5, 1.0, ((0, 4),)),
        "w_gate": bell_draw(key_list[9], (D, FF), D ** -0.5, 0.1875, ((1, 4),)),
        "w_up": bell_draw(key_list[10], (D, FF), D ** -0.5, 0.1875, ((1, 4),)),
        "w_down": bell_draw(key_list[11], (FF, D), FF ** -0.5, 0.109375, ((0, 4),)),
        "gain_attn": jnp.clip(1.0 + 0.1 * jax.random.normal(key_list[12], (D,), jnp.float32), 0.5, 1.5),
        "gain_mlp": jnp.clip(1.0 + 0.1 * jax.random.normal(key_list[13], (D,), jnp.float32), 0.5, 1.5),
        "out_cotangent": bell_draw(key_list[14], (TOKENS, D), 1.0, 6.0, ((0, 8),)),
    }


@jax.custom_vjp
def low(v):
    return lax.optimization_barrier(v.astype(jnp.bfloat16)).astype(jnp.float32)

@jax.custom_vjp
def low_back(v):
    return v

def low_keep(v):
    return (low(v), None)

def low_pass(kept, grad):
    return (grad,)

def back_keep(v):
    return (v, None)

def back_low(kept, grad):
    return (low(grad),)
low.defvjp(low_keep, low_pass)
low_back.defvjp(back_keep, back_low)
norm_eps = 1e-06

def token_places(segment_ids):
    n_tokens = segment_ids.shape[0]
    indices = jnp.arange(n_tokens, dtype=jnp.int32)
    starts_new = jnp.concatenate([jnp.ones((1,), jnp.bool_), segment_ids[1:] != segment_ids[:-1]])
    begins = lax.cummax(jnp.where(starts_new, indices, jnp.zeros_like(indices)), axis=0)
    return indices - begins

def rotate(values, places, turn_sign):
    half_size = values.shape[-1] // 2
    frequency = jnp.exp(jnp.arange(half_size, dtype=jnp.float32) * (-2.0 * math.log(10000.0) / values.shape[-1]))
    angles = places.astype(jnp.float32)[:, None] * frequency[None, :]
    cosine = jnp.cos(angles)[:, None, :]
    sine_part = turn_sign * jnp.sin(angles)[:, None, :]
    first_half = values[..., :half_size]
    second_half = values[..., half_size:]
    return jnp.concatenate([first_half * cosine - second_half * sine_part, second_half * cosine + first_half * sine_part], -1)

def rms_norm(values, gain_vec):
    return values * lax.rsqrt(lax.optimization_barrier(jnp.mean(values * values, axis=-1, keepdims=True)) + norm_eps) * gain_vec

def highest_dot(left, right):
    return jnp.dot(left, right, precision=lax.Precision.HIGHEST)

def attend(packed):
    queries, key_rows, blended, seg_rows, live_rows = packed
    scores = jnp.einsum('qhd,khd->hqk', queries, key_rows, precision=lax.Precision.HIGHEST) * HD ** (-0.5)
    scores = low_back(scores)
    place = jnp.arange(SEQ, dtype=jnp.int32)
    allowed = (seg_rows[:, None] == seg_rows[None, :]) & (place[None, :] <= place[:, None])
    allowed = allowed & ((live_rows[None, :] == 1) | (place[None, :] == place[:, None]))
    scores = jnp.where(allowed[None], scores, -1e+30)
    row_peak = lax.optimization_barrier(jnp.max(scores, -1, keepdims=True))
    exp_scores = jnp.exp(scores - row_peak)
    probs = exp_scores / lax.optimization_barrier(jnp.sum(exp_scores, -1, keepdims=True))
    return jnp.einsum('hqk,khd->qhd', low(probs), blended, precision=lax.Precision.HIGHEST)

def reference(hidden_in, first_in, segment_ids, valid_tokens, w_query, w_key, w_value, w_first_value, w_out, w_gate, w_up, w_down, gain_attn, gain_mlp, out_cotangent):
    n_tokens = hidden_in.shape[0]
    n_seqs = n_tokens // SEQ
    places = token_places(segment_ids)
    live_rows = valid_tokens.astype(jnp.float32)

    def forward(x_float, first_float, wq_f, wk_f, wv_f, wv1_f, wo_f, wg_f, wu_f, wd_f, gain_one, gain_two):
        h_one = low(rms_norm(x_float, gain_one))
        queries = low(rotate(low_back(highest_dot(h_one, wq_f)).reshape(n_tokens, H, HD), places, 1.0))
        key_rows = low(rotate(low_back(highest_dot(h_one, wk_f)).reshape(n_tokens, H, HD), places, 1.0))
        first_values = low(highest_dot(first_float, wv1_f))
        blended = low(low_back(0.5 * highest_dot(h_one, wv_f) + 0.5 * first_values))
        attended = lax.map(jax.checkpoint(attend), (queries.reshape(n_seqs, SEQ, H, HD), key_rows.reshape(n_seqs, SEQ, H, HD), blended.reshape(n_seqs, SEQ, H, HD), segment_ids.reshape(n_seqs, SEQ), valid_tokens.reshape(n_seqs, SEQ)))
        attn_mixed = low(low_back(attended.reshape(n_tokens, D) * live_rows[:, None]))
        residual = x_float + low_back(highest_dot(attn_mixed, wo_f))
        h_two = low(rms_norm(residual, gain_two))
        gate_pre = low_back(highest_dot(h_two, wg_f))
        up_pre = low_back(highest_dot(h_two, wu_f))
        ffn_hidden = low(low_back(jax.nn.silu(gate_pre) * up_pre))
        return (residual + highest_dot(ffn_hidden, wd_f), (first_values, blended))
    floats = (hidden_in, first_in, w_query, w_key, w_value, w_first_value, w_out, w_gate, w_up, w_down, gain_attn, gain_mlp)
    floats = tuple((item.astype(jnp.float32) for item in floats))
    block_float, pullback, extras = jax.vjp(forward, *floats, has_aux=True)
    grads = pullback(out_cotangent.astype(jnp.float32))
    first_values, blended = extras
    return (block_float.astype(jnp.bfloat16), grads[0].astype(jnp.bfloat16), grads[2], grads[3], grads[4], grads[5], grads[6], grads[7], grads[8], grads[9], grads[10], grads[11], jnp.mean(first_values * first_values), jnp.mean(blended * blended))
```

```python
import functools
import math

import jax
import jax.numpy as jnp
from jax import lax
from jax.experimental import pallas as pl
from jax.experimental.pallas import tpu as pltpu
from jax.sharding import PartitionSpec as P

HD = 64
SEQ = 2048
QB = 256


norm_eps = 1e-06


def token_places(segment_ids):
    n_tokens = segment_ids.shape[0]
    indices = jnp.arange(n_tokens, dtype=jnp.int32)
    starts_new = jnp.concatenate([jnp.ones((1,), jnp.bool_), segment_ids[1:] != segment_ids[:-1]])
    begins = lax.cummax(jnp.where(starts_new, indices, jnp.zeros_like(indices)), axis=0)
    return indices - begins


def rotate(values, places, turn_sign):
    half_size = values.shape[-1] // 2
    frequency = jnp.exp(
        jnp.arange(half_size, dtype=jnp.float32) * (-2.0 * math.log(10000.0) / values.shape[-1])
    )
    angles = places.astype(jnp.float32)[:, None] * frequency[None, :]
    cosine = jnp.cos(angles)[:, None, :]
    sine_part = turn_sign * jnp.sin(angles)[:, None, :]
    first_half = values[..., :half_size]
    second_half = values[..., half_size:]
    return jnp.concatenate(
        [
            first_half * cosine - second_half * sine_part,
            second_half * cosine + first_half * sine_part,
        ],
        -1,
    )


def rms_parts(values):
    inverse = lax.rsqrt(jnp.mean(values * values, axis=-1, keepdims=True) + norm_eps)
    return (values * inverse, inverse)


def rms_back(grad_rows, normed, inverse, gain_vec):
    grad_normed = grad_rows * gain_vec
    return inverse * (grad_normed - normed * jnp.mean(grad_normed * normed, axis=-1, keepdims=True))


def dot(a, b, ca, cb):
    return lax.dot_general(a, b, (((ca,), (cb,)), ((), ())), preferred_element_type=jnp.float32)


def pair_lane(shape, head):
    lane = lax.broadcasted_iota(jnp.int32, shape, 1)
    return (lane < 64) if head == 0 else (lane >= 64)


def attend_kernel(order_ref, start_ref, q_ref, k_ref, v_ref, o_ref, lse_ref, *, pieces, rows):
    z = order_ref[0]
    subs = rows // QB
    for j in range(pieces):
        zj = jnp.bitwise_xor(z, j)
        for sub in range(subs):
            first = j * rows + sub * QB
            q_pair = q_ref[zj, sub * QB:(sub + 1) * QB, :]
            start = start_ref[0:1, first:first + QB]
            q_pos = first + lax.broadcasted_iota(jnp.int32, (1, QB), 1)
            outs = []
            for head in range(2):
                qm = jnp.where(pair_lane(q_pair.shape, head), q_pair, jnp.zeros_like(q_pair))
                blocks = []
                for i in range(j + 1):
                    zi = jnp.bitwise_xor(z, i)
                    n = rows if i < j else (sub + 1) * QB
                    s = dot(k_ref[zi, :n, :], qm, 1, 1)
                    k_pos = i * rows + lax.broadcasted_iota(jnp.int32, (n, QB), 0)
                    keep = k_pos >= start
                    if i == j:
                        keep = keep & (k_pos <= q_pos)
                    blocks.append((zi, n, jnp.where(keep, s, -1e30)))
                peak = functools.reduce(jnp.maximum, [jnp.max(b[2], 0, keepdims=True) for b in blocks])
                total = 0.0
                acc = 0.0
                for zi, n, s in blocks:
                    p = jnp.exp(s - peak)
                    total = total + jnp.sum(p, 0, keepdims=True)
                    acc = acc + dot(v_ref[zi, :n, :], p.astype(jnp.bfloat16), 0, 0)
                outs.append((acc / total)[head * 64:(head + 1) * 64])
                lse_ref[0, head:head + 1, first:first + QB] = peak + jnp.log(total)
            o_ref[zj, sub * QB:(sub + 1) * QB, :] = jnp.transpose(jnp.concatenate(outs, 0)).astype(o_ref.dtype)


def attend(order, start, q, k, v, vmem=48 * 2**20):
    pieces, rows, width = q.shape
    pairs = width // 128
    blk = pl.BlockSpec((pieces, rows, 128), lambda p, *_: (0, 0, p))
    return pl.pallas_call(
        functools.partial(attend_kernel, pieces=pieces, rows=rows),
        grid_spec=pltpu.PrefetchScalarGridSpec(
            num_scalar_prefetch=1, grid=(pairs,),
            in_specs=[pl.BlockSpec((1, pieces * rows), lambda p, *_: (0, 0)), blk, blk, blk],
            out_specs=[blk, pl.BlockSpec((1, 2, pieces * rows), lambda p, *_: (p, 0, 0))],
        ),
        out_shape=[jax.ShapeDtypeStruct(q.shape, jnp.bfloat16),
                   jax.ShapeDtypeStruct((pairs, 2, pieces * rows), jnp.float32)],
        compiler_params=pltpu.CompilerParams(vmem_limit_bytes=vmem),
        cost_estimate=pl.CostEstimate(flops=2 * 2 * (pieces * rows)**2 * width, bytes_accessed=8 * pieces * rows * width, transcendentals=pieces * rows * pieces * rows * pairs),
    )(order, start, q, k, v)


def back_kernel(order_ref, start_ref, q_ref, k_ref, v_ref, o_ref, g_ref, lse_ref, dq_ref, dk_ref, dv_ref, acc_k, acc_v, *, pieces, rows):
    z = order_ref[0]
    subs = rows // QB
    acc_k[...] = jnp.zeros_like(acc_k)
    acc_v[...] = jnp.zeros_like(acc_v)
    for j in range(pieces):
        zj = jnp.bitwise_xor(z, j)
        for sub in range(subs):
            first = j * rows + sub * QB
            here = slice(sub * QB, (sub + 1) * QB)
            q_pair = q_ref[zj, here, :]
            g_pair = g_ref[zj, here, :]
            start = start_ref[0:1, first:first + QB]
            q_pos = first + lax.broadcasted_iota(jnp.int32, (1, QB), 1)
            inner = jnp.transpose(o_ref[zj, here, :].astype(jnp.float32) * g_pair.astype(jnp.float32))
            outs = []
            for head in range(2):
                mine = pair_lane(q_pair.shape, head)
                qm = jnp.where(mine, q_pair, jnp.zeros_like(q_pair))
                gm = jnp.where(mine, g_pair, jnp.zeros_like(g_pair))
                delta = jnp.sum(inner[head * 64:(head + 1) * 64], 0, keepdims=True)
                lse = lse_ref[0, head:head + 1, first:first + QB]
                acc = 0.0
                for i in range(j + 1):
                    zi = jnp.bitwise_xor(z, i)
                    n = rows if i < j else (sub + 1) * QB
                    k_blk = k_ref[zi, :n, :]
                    s = dot(k_blk, qm, 1, 1)
                    k_pos = i * rows + lax.broadcasted_iota(jnp.int32, (n, QB), 0)
                    keep = k_pos >= start
                    if i == j:
                        keep = keep & (k_pos <= q_pos)
                    p = jnp.exp(jnp.where(keep, s, -1e30) - lse)
                    dp = dot(v_ref[zi, :n, :], gm, 1, 1)
                    ds = (p * (dp - delta)).astype(jnp.bfloat16)
                    acc_v[i, :n, :] += dot(p.astype(jnp.bfloat16), gm, 1, 0)
                    acc_k[i, :n, :] += dot(ds, qm, 1, 0)
                    acc = acc + dot(k_blk, ds, 0, 0)
                outs.append(acc[head * 64:(head + 1) * 64])
            dq_ref[zj, here, :] = (jnp.transpose(jnp.concatenate(outs, 0)) * 0.125).astype(dq_ref.dtype)
    for j in range(pieces):
        zj = jnp.bitwise_xor(z, j)
        dk_ref[zj] = acc_k[j].astype(dk_ref.dtype)
        dv_ref[zj] = acc_v[j].astype(dv_ref.dtype)


def attend_back(order, start, q, k, v, o, g, lse, vmem=48 * 2**20, dt=jnp.bfloat16):
    pieces, rows, width = q.shape
    pairs = width // 128
    blk = pl.BlockSpec((pieces, rows, 128), lambda p, *_: (0, 0, p))
    return pl.pallas_call(
        functools.partial(back_kernel, pieces=pieces, rows=rows),
        grid_spec=pltpu.PrefetchScalarGridSpec(
            num_scalar_prefetch=1, grid=(pairs,),
            in_specs=[pl.BlockSpec((1, pieces * rows), lambda p, *_: (0, 0)), blk, blk, blk, blk, blk,
                      pl.BlockSpec((1, 2, pieces * rows), lambda p, *_: (p, 0, 0))],
            out_specs=[blk, blk, blk],
            scratch_shapes=[pltpu.VMEM((pieces, rows, 128), jnp.float32)] * 2,
        ),
        out_shape=[jax.ShapeDtypeStruct(q.shape, dt)] * 3,
        compiler_params=pltpu.CompilerParams(vmem_limit_bytes=vmem),
        cost_estimate=pl.CostEstimate(flops=2 * 5 * (pieces * rows)**2 * width, bytes_accessed=20 * pieces * rows * width, transcendentals=pieces * rows * pieces * rows * pairs),
    )(order, start, q, k, v, o, g, lse)


def shards(
    hidden_in,
    first_in,
    segment_ids,
    valid_tokens,
    w_query,
    w_key,
    w_value,
    w_first_value,
    w_out,
    w_gate,
    w_up,
    w_down,
    gain_attn,
    gain_mlp,
    out_cotangent,
):
    own_rows = hidden_in.shape[0]
    n_tokens = segment_ids.shape[0]
    head_cols = w_query.shape[1]
    local_heads = head_cols // HD
    ffn_cols = w_gate.shape[1]
    places = token_places(segment_ids)
    live_rows = valid_tokens.astype(jnp.float32)[:, None]
    x_float = hidden_in.astype(jnp.float32)
    normed_one, inverse_one = rms_parts(x_float)
    normed_all = lax.all_gather(
        (normed_one * gain_attn).astype(jnp.bfloat16), "mp", axis=0, tiled=True
    )
    w_inner = jnp.concatenate([w_query, w_key, w_value], 1)
    projected = jnp.dot(normed_all, w_inner, preferred_element_type=jnp.float32)
    queries = rotate(
        projected[:, :head_cols].reshape(n_tokens, local_heads, HD), places, 1.0
    ).astype(jnp.bfloat16)
    key_rows = rotate(
        projected[:, head_cols : 2 * head_cols].reshape(n_tokens, local_heads, HD), places, 1.0
    ).astype(jnp.bfloat16)
    first_all = lax.all_gather(first_in, "mp", axis=0, tiled=True)
    first_values = jnp.dot(first_all, w_first_value, preferred_element_type=jnp.float32).astype(
        jnp.bfloat16
    )
    blended = (0.5 * projected[:, 2 * head_cols :] + 0.5 * first_values.astype(jnp.float32)).astype(
        jnp.bfloat16
    )
    first_key = jnp.where(valid_tokens == 1, jnp.arange(n_tokens, dtype=jnp.int32) - places, jnp.arange(n_tokens, dtype=jnp.int32))[None]
    order = jnp.zeros((1,), jnp.int32)
    cut = lambda a: a.reshape(4, n_tokens // 4, head_cols)
    q_cut, k_cut, v_cut = cut(queries * jnp.bfloat16(0.125)), cut(key_rows), cut(blended)
    attended, logsum = attend(order, first_key, q_cut, k_cut, v_cut)
    attn_mixed = (attended.reshape(n_tokens, head_cols).astype(jnp.float32) * live_rows).astype(jnp.bfloat16)
    residual = x_float + lax.psum_scatter(
        jnp.dot(attn_mixed, w_out, preferred_element_type=jnp.float32),
        "mp",
        scatter_dimension=0,
        tiled=True,
    )
    normed_two, inverse_two = rms_parts(residual)
    mid_all = lax.all_gather((normed_two * gain_mlp).astype(jnp.bfloat16), "mp", axis=0, tiled=True)
    w_gate_up = jnp.concatenate([w_gate, w_up], 1)
    gate_up = jnp.dot(mid_all, w_gate_up, preferred_element_type=jnp.float32)
    gate_pre = gate_up[:, :ffn_cols]
    up_pre = gate_up[:, ffn_cols:]
    gate_sigmoid = jax.nn.sigmoid(gate_pre)
    silu_value = gate_pre * gate_sigmoid
    ffn_hidden = (silu_value * up_pre).astype(jnp.bfloat16)
    block_out = (
        residual
        + lax.psum_scatter(
            jnp.dot(ffn_hidden, w_down, preferred_element_type=jnp.float32).astype(jnp.bfloat16),
            "mp",
            scatter_dimension=0,
            tiled=True,
        ).astype(jnp.float32)
    ).astype(jnp.bfloat16)
    grad_rows = lax.dynamic_slice_in_dim(
        out_cotangent, lax.axis_index("mp") * own_rows, own_rows, 0
    ).astype(jnp.float32)
    grad_down = jnp.einsum(
        "tf,td->fd", ffn_hidden, out_cotangent, preferred_element_type=jnp.float32
    )
    grad_hidden = (
        jnp.einsum("td,fd->tf", out_cotangent, w_down, preferred_element_type=jnp.float32)
        .astype(jnp.bfloat16)
        .astype(jnp.float32)
    )
    grad_gate_pre = (
        grad_hidden * up_pre * gate_sigmoid * (1.0 + gate_pre * (1.0 - gate_sigmoid))
    ).astype(jnp.bfloat16)
    grad_up_pre = (grad_hidden * silu_value).astype(jnp.bfloat16)
    grad_gate_up = jnp.concatenate([grad_gate_pre, grad_up_pre], 1)
    grad_w_gate_up = jnp.einsum(
        "td,tf->df", mid_all, grad_gate_up, preferred_element_type=jnp.float32
    )
    grad_mid = lax.psum_scatter(
        jnp.einsum("tf,df->td", grad_gate_up, w_gate_up, preferred_element_type=jnp.float32).astype(
            jnp.bfloat16
        ),
        "mp",
        scatter_dimension=0,
        tiled=True,
    ).astype(jnp.float32)
    grad_resid = grad_rows + rms_back(grad_mid, normed_two, inverse_two, gain_mlp)
    part_gain_mlp = jnp.sum(grad_mid * normed_two, 0)
    grad_attn_all = lax.all_gather(grad_resid.astype(jnp.bfloat16), "mp", axis=0, tiled=True)
    grad_w_out = jnp.einsum(
        "tw,td->wd", attn_mixed, grad_attn_all, preferred_element_type=jnp.float32
    )
    grad_attn_rounded = jnp.einsum(
        "td,wd->tw", grad_attn_all, w_out, preferred_element_type=jnp.float32
    ).astype(jnp.bfloat16)
    grad_mixed = (grad_attn_rounded.astype(jnp.float32) * live_rows).astype(jnp.bfloat16)
    grad_queries, grad_keys, grad_values = attend_back(
        order, first_key, q_cut, k_cut, v_cut, attended, cut(grad_mixed), logsum
    )
    grad_queries = grad_queries.astype(jnp.float32).reshape(n_tokens, local_heads, HD)
    grad_keys = grad_keys.astype(jnp.float32).reshape(n_tokens, local_heads, HD)
    grad_blend = grad_values.reshape(n_tokens, head_cols).astype(jnp.bfloat16)
    grad_half = (grad_blend.astype(jnp.float32) * 0.5).astype(jnp.bfloat16)
    grad_query_pre = (
        rotate(grad_queries, places, -1.0).reshape(n_tokens, head_cols).astype(jnp.bfloat16)
    )
    grad_key_pre = rotate(grad_keys, places, -1.0).reshape(n_tokens, head_cols).astype(jnp.bfloat16)
    grad_projected = jnp.concatenate([grad_query_pre, grad_key_pre, grad_half], 1)
    grad_w_inner = jnp.einsum(
        "td,tc->dc", normed_all, grad_projected, preferred_element_type=jnp.float32
    )
    grad_normed = lax.psum_scatter(
        jnp.einsum("tc,dc->td", grad_projected, w_inner, preferred_element_type=jnp.float32).astype(
            jnp.bfloat16
        ),
        "mp",
        scatter_dimension=0,
        tiled=True,
    ).astype(jnp.float32)
    grad_input = (grad_resid + rms_back(grad_normed, normed_one, inverse_one, gain_attn)).astype(
        jnp.bfloat16
    )
    part_gain_attn = jnp.sum(grad_normed * normed_one, 0)
    grad_first = jnp.einsum("td,tc->dc", first_all, grad_half, preferred_element_type=jnp.float32)
    summed = (
        lax.psum(grad_w_inner.astype(jnp.bfloat16), "dp").astype(jnp.float32),
        lax.psum(grad_first.astype(jnp.bfloat16), "dp").astype(jnp.float32),
        lax.psum(grad_w_out.astype(jnp.bfloat16), "dp").astype(jnp.float32),
        lax.psum(grad_w_gate_up.astype(jnp.bfloat16), "dp").astype(jnp.float32),
        lax.psum(grad_down.astype(jnp.bfloat16), "dp").astype(jnp.float32),
    )
    first_float = first_values.astype(jnp.float32)
    blend_float = blended.astype(jnp.float32)
    small_totals = lax.psum(
        (
            part_gain_attn,
            part_gain_mlp,
            jnp.sum(first_float * first_float),
            jnp.sum(blend_float * blend_float),
        ),
        ("dp", "mp"),
    )
    element_count = float(n_tokens * lax.axis_size("dp") * hidden_in.shape[1])
    inner_sum = summed[0]
    gate_up_sum = summed[3]
    return (
        block_out,
        grad_input,
        inner_sum[:, :head_cols],
        inner_sum[:, head_cols : 2 * head_cols],
        inner_sum[:, 2 * head_cols :],
        summed[1],
        summed[2],
        gate_up_sum[:, :ffn_cols],
        gate_up_sum[:, ffn_cols:],
        summed[4],
        small_totals[0],
        small_totals[1],
        small_totals[2] / element_count,
        small_totals[3] / element_count,
    )


def solution(mesh):
    placed = (
        P(("dp", "mp"), None),
        P(("dp", "mp"), None),
        P("dp"),
        P("dp"),
        P(None, "mp"),
        P(None, "mp"),
        P(None, "mp"),
        P(None, "mp"),
        P("mp", None),
        P(None, "mp"),
        P(None, "mp"),
        P("mp", None),
        P(),
        P(),
        P("dp", None),
    )
    return jax.shard_map(
        shards,
        mesh=mesh,
        in_specs=placed,
        out_specs=(
            P(("dp", "mp"), None),
            P(("dp", "mp"), None),
            P(None, "mp"),
            P(None, "mp"),
            P(None, "mp"),
            P(None, "mp"),
            P("mp", None),
            P(None, "mp"),
            P(None, "mp"),
            P("mp", None),
            P(),
            P(),
            P(),
            P(),
        ),
        check_vma=False,
    )
```

```python
import functools
import math

import jax
import jax.numpy as jnp
from jax import lax
from jax.experimental import pallas as pl
from jax.experimental.pallas import tpu as pltpu
from jax.sharding import PartitionSpec as P

HD = 64
norm_eps = 1e-06


def token_places(segment_ids):
    n_tokens = segment_ids.shape[0]
    indices = jnp.arange(n_tokens, dtype=jnp.int32)
    starts_new = jnp.concatenate([jnp.ones((1,), jnp.bool_), segment_ids[1:] != segment_ids[:-1]])
    begins = lax.cummax(jnp.where(starts_new, indices, jnp.zeros_like(indices)), axis=0)
    return indices - begins


QB = 256
VMEM = 48 * 2**20


def dot(a, b, ca, cb):
    return lax.dot_general(a, b, (((ca,), (cb,)), ((), ())), preferred_element_type=jnp.float32)


def lane_of(shape):
    return lax.broadcasted_iota(jnp.int32, shape, 1)


def turned(values, cosine, sine):
    near = lane_of(values.shape) % HD < HD // 2
    swapped = jnp.where(near, pltpu.roll(values, 128 - HD // 2, 1), pltpu.roll(values, HD // 2, 1))
    return values * cosine + swapped * sine


def project_kernel(h_ref, first_ref, w_ref, cos_ref, sin_ref, out_ref, power_ref):
    h, first = h_ref[...], first_ref[...]
    cosine, sine = cos_ref[...], sin_ref[...]
    at = pl.program_id(0)

    @pl.when(at == 0)
    def _():
        power_ref[...] = jnp.zeros_like(power_ref)

    for half in range(2):
        base = half * 512
        qkv = dot(h, w_ref[:, base : base + 384], 1, 0)
        raw = dot(first, w_ref[:, base + 384 : base + 512], 1, 0).astype(jnp.bfloat16).astype(jnp.float32)
        out_ref[half, :, 0:128] = turned(qkv[:, 0:128], cosine, sine).astype(jnp.bfloat16) * jnp.bfloat16(0.125)
        out_ref[half, :, 128:256] = turned(qkv[:, 128:256], cosine, sine).astype(jnp.bfloat16)
        blend = (0.5 * qkv[:, 256:384] + 0.5 * raw).astype(jnp.bfloat16)
        out_ref[half, :, 256:384] = blend
        blend = blend.astype(jnp.float32)
        power_ref[0:1, :] += jnp.sum(raw * raw, 0, keepdims=True)
        power_ref[1:2, :] += jnp.sum(blend * blend, 0, keepdims=True)


def project(h, first, weight, cosine, sine):
    n, width = h.shape
    rows = n // 2
    subs = rows // QB
    return pl.pallas_call(
        project_kernel,
        grid=(n // QB,),
        in_specs=[
            pl.BlockSpec((QB, width), lambda i: (i, 0)),
            pl.BlockSpec((QB, width), lambda i: (i, 0)),
            pl.BlockSpec(weight.shape, lambda i: (0, 0)),
            pl.BlockSpec((QB, 128), lambda i: (i, 0)),
            pl.BlockSpec((QB, 128), lambda i: (i, 0)),
        ],
        out_specs=[
            pl.BlockSpec((2, QB, 384), lambda i: (i // subs, i % subs, 0)),
            pl.BlockSpec((8, 128), lambda i: (0, 0)),
        ],
        out_shape=[
            jax.ShapeDtypeStruct((4, rows, 384), jnp.bfloat16),
            jax.ShapeDtypeStruct((8, 128), jnp.float32),
        ],
        compiler_params=pltpu.CompilerParams(vmem_limit_bytes=VMEM),
        cost_estimate=pl.CostEstimate(
            flops=2 * n * width * 1024, bytes_accessed=2 * width * (2 * n + 1024), transcendentals=0
        ),
    )(h, first, weight, cosine, sine)


def causal(scores, start, q_pos, i, rows, last):
    k_pos = i * rows + lax.broadcasted_iota(jnp.int32, scores.shape, 0)
    keep = k_pos >= start
    if last:
        keep = keep & (k_pos <= q_pos)
    return jnp.where(keep, scores, -1e30)


def attend_kernel(start_ref, q_ref, k_ref, v_ref, o_ref, lse_ref, *, pieces, rows):
    for j in range(pieces):
        for sub in range(rows // QB):
            first = j * rows + sub * QB
            q_pair = q_ref[j, sub * QB : (sub + 1) * QB, :]
            start = start_ref[0:1, first : first + QB]
            q_pos = first + lane_of((1, QB))
            outs = []
            for head in range(2):
                mine = lane_of(q_pair.shape) // HD == head
                qm = jnp.where(mine, q_pair, jnp.zeros_like(q_pair))
                blocks = []
                for i in range(j + 1):
                    n = rows if i < j else (sub + 1) * QB
                    s = dot(k_ref[i, :n, :], qm, 1, 1)
                    blocks.append((i, n, causal(s, start, q_pos, i, rows, i == j)))
                peak = functools.reduce(jnp.maximum, [jnp.max(b[2], 0, keepdims=True) for b in blocks])
                total = 0.0
                acc = 0.0
                for i, n, s in blocks:
                    p = jnp.exp(s - peak)
                    total = total + jnp.sum(p, 0, keepdims=True)
                    acc = acc + dot(v_ref[i, :n, :], p.astype(jnp.bfloat16), 0, 0)
                outs.append((acc / total)[head * HD : (head + 1) * HD])
                lse_ref[head : head + 1, first : first + QB] = peak + jnp.log(total)
            o_ref[j, sub * QB : (sub + 1) * QB, :] = jnp.transpose(jnp.concatenate(outs, 0)).astype(o_ref.dtype)


def column(pieces, rows, at):
    return pl.BlockSpec((pieces, rows, 128), lambda _: (0, 0, at))


def whole(shape):
    return pl.BlockSpec(shape, lambda _: (0,) * len(shape))


def attend(start, qkv):
    pieces, rows, _ = qkv.shape
    n = pieces * rows
    return pl.pallas_call(
        functools.partial(attend_kernel, pieces=pieces, rows=rows),
        grid=(1,),
        in_specs=[whole((1, n))] + [column(pieces, rows, i) for i in range(3)],
        out_specs=[whole((pieces, rows, 128)), whole((2, n))],
        out_shape=[
            jax.ShapeDtypeStruct((pieces, rows, 128), jnp.bfloat16),
            jax.ShapeDtypeStruct((2, n), jnp.float32),
        ],
        compiler_params=pltpu.CompilerParams(vmem_limit_bytes=VMEM),
        cost_estimate=pl.CostEstimate(flops=8 * n * n * 128, bytes_accessed=8 * n * 128, transcendentals=n * n),
    )(start, qkv, qkv, qkv)


def back_kernel(
    start_ref, q_ref, k_ref, v_ref, o_ref, g_ref, lse_ref, flat_ref, cos_ref, sin_ref, d_ref, acc_k, acc_v, *, pieces, rows
):
    acc_k[...] = jnp.zeros_like(acc_k)
    acc_v[...] = jnp.zeros_like(acc_v)
    low = HD // 2
    for j in range(pieces):
        for sub in range(rows // QB):
            first = j * rows + sub * QB
            here = slice(sub * QB, (sub + 1) * QB)
            q_pair = q_ref[j, here, :]
            g_pair = g_ref[j, here, :]
            start = start_ref[0:1, first : first + QB]
            q_pos = first + lane_of((1, QB))
            inner = jnp.transpose(o_ref[j, here, :].astype(jnp.float32) * g_pair.astype(jnp.float32))
            cosine = flat_ref[0, :, first : first + QB]
            sine = flat_ref[1, :, first : first + QB]
            outs = []
            for head in range(2):
                mine = lane_of(q_pair.shape) // HD == head
                qm = jnp.where(mine, q_pair, jnp.zeros_like(q_pair))
                gm = jnp.where(mine, g_pair, jnp.zeros_like(g_pair))
                delta = jnp.sum(inner[head * HD : (head + 1) * HD], 0, keepdims=True)
                lse = lse_ref[head : head + 1, first : first + QB]
                acc = 0.0
                for i in range(j + 1):
                    n = rows if i < j else (sub + 1) * QB
                    k_blk = k_ref[i, :n, :]
                    s = causal(dot(k_blk, qm, 1, 1), start, q_pos, i, rows, i == j)
                    p = jnp.exp(s - lse)
                    dp = dot(v_ref[i, :n, :], gm, 1, 1)
                    ds = (p * (dp - delta)).astype(jnp.bfloat16)
                    acc_v[i, :n, :] += dot(p.astype(jnp.bfloat16), gm, 1, 0)
                    acc_k[i, :n, :] += dot(ds, qm, 1, 0)
                    acc = acc + dot(k_blk, ds, 0, 0)
                near = acc[head * HD : head * HD + low] * 0.125
                far = acc[head * HD + low : (head + 1) * HD] * 0.125
                outs += [near * cosine + far * sine, far * cosine - near * sine]
            d_ref[j, here, 0:128] = jnp.transpose(jnp.concatenate(outs, 0)).astype(d_ref.dtype)
    for j in range(pieces):
        here = slice(j * rows, (j + 1) * rows)
        d_ref[j, :, 128:256] = turned(acc_k[j], cos_ref[here, :], -sin_ref[here, :]).astype(d_ref.dtype)
        d_ref[j, :, 256:384] = acc_v[j].astype(d_ref.dtype) * jnp.bfloat16(0.5)


def attend_back(start, qkv, o, g, lse, flat, cosine, sine):
    pieces, rows, _ = qkv.shape
    n = pieces * rows
    one = whole((pieces, rows, 128))
    return pl.pallas_call(
        functools.partial(back_kernel, pieces=pieces, rows=rows),
        grid=(1,),
        in_specs=[whole((1, n))]
        + [column(pieces, rows, i) for i in range(3)]
        + [one, one, whole((2, n)), whole(flat.shape), whole((n, 128)), whole((n, 128))],
        out_specs=whole((pieces, rows, 384)),
        scratch_shapes=[pltpu.VMEM((pieces, rows, 128), jnp.float32)] * 2,
        out_shape=jax.ShapeDtypeStruct((pieces, rows, 384), jnp.bfloat16),
        compiler_params=pltpu.CompilerParams(vmem_limit_bytes=VMEM),
        cost_estimate=pl.CostEstimate(flops=20 * n * n * 128, bytes_accessed=20 * n * 128, transcendentals=n * n),
    )(start, qkv, qkv, qkv, o, g, lse, flat, cosine, sine)


def moved(values, bit):
    return lax.ppermute(values, "dp", [(i, i ^ bit) for i in range(lax.axis_size("dp"))])


def cross_pairs(n_dp):
    pairs = []
    for d in range(n_dp):
        for z in range(4):
            pairs.append((d * 4 + z, d * 4 + (z ^ 1) if z // 2 == d % 2 else (d ^ 1) * 4 + (z ^ 2)))
    return pairs


def side_pairs(n_dp):
    return [(d * 4 + z, d * 4 + (z ^ 1)) for d in range(n_dp) for z in range(4) if z // 2 != d % 2]


def tied(values, *others):
    return lax.optimization_barrier((values, others))[0]


class Place:
    def __init__(self):
        self.n_dp = lax.axis_size("dp")
        self.slots = self.n_dp // 2
        self.d = lax.axis_index("dp")
        self.z = lax.axis_index("mp")
        self.core = self.d % 2
        self.slot = self.d // 2
        self.own = (self.z // 2) == self.core
        self.even = (self.z % 2) == 0
        self.sides = [[2 * i + c for i in range(self.slots)] for c in range(2)]

    def cross(self, values):
        return lax.ppermute(values, ("dp", "mp"), cross_pairs(self.n_dp))

    def side(self, values):
        return lax.ppermute(values, ("dp", "mp"), side_pairs(self.n_dp))

    def ordered(self, mine, other):
        return jnp.where(self.core == 0, jnp.concatenate([mine, other], 0), jnp.concatenate([other, mine], 0))

    def slice_of(self, weight):
        rows = weight.shape[0] // self.slots
        return lax.dynamic_slice_in_dim(weight, self.slot * rows, rows, 0)

    def quarters(self, part):
        got = self.cross(part)
        far = self.side(got)
        first = jnp.where(self.own, part, got)
        second = jnp.where(self.own, got, far)
        return jnp.where(self.even, first, second), jnp.where(self.even, second, first)

    def gathered(self, part):
        return lax.all_gather(part, "dp", axis=0, tiled=True, axis_index_groups=self.sides)

    def gathered_direct(self, part):
        if self.slots != 4:
            return self.gathered(part)
        rows = part.shape[0]
        whole_part = jnp.zeros((4 * rows, part.shape[1]), part.dtype)
        for k, piece in enumerate((part, moved(part, 2), moved(part, 4), moved(part, 6))):
            whole_part = lax.dynamic_update_slice_in_dim(whole_part, piece, (self.slot ^ k) * rows, 0)
        return whole_part

    def scattered(self, values):
        return lax.psum_scatter(values, "dp", scatter_dimension=0, tiled=True, axis_index_groups=self.sides)

    def scattered_direct(self, values):
        if self.slots != 4:
            return self.scattered(values)
        rows = values.shape[0] // 4
        pick = lambda k: lax.dynamic_slice_in_dim(values, (self.slot ^ k) * rows, rows, 0)
        parts = [pick(0), moved(pick(1), 2), moved(pick(2), 4), moved(pick(3), 6)]
        return sum(p.astype(jnp.float32) for p in parts).astype(jnp.bfloat16)

    def returned(self, low, high):
        f32, bf16 = jnp.float32, jnp.bfloat16
        rows = low.shape[0]
        first = jnp.where(self.even, low, high)
        second = jnp.where(self.even, high, low)
        total = (first.astype(f32) + self.side(second).astype(f32)).astype(bf16)
        got = self.cross(jnp.where(self.own, second, total))
        part = jnp.where(self.own, (first.astype(f32) + got.astype(f32)).astype(bf16), got)
        half = rows // 2
        cut = lambda which: lax.dynamic_slice_in_dim(part, which * half, half, 0)
        done = (cut(self.core).astype(f32) + moved(cut(1 - self.core), 1).astype(f32)).astype(bf16)
        return lax.all_gather(done, "dp", axis=0, tiled=True)


def exchanged(values):
    return lax.all_to_all(values, "mp", 0, 0, tiled=True)


def rms_parts(values):
    inverse = lax.rsqrt(jnp.mean(values * values, axis=-1, keepdims=True) + norm_eps)
    return (values * inverse, inverse)


def rms_back(grad_rows, normed, inverse, gain_vec):
    grad_normed = grad_rows * gain_vec
    return inverse * (grad_normed - normed * jnp.mean(grad_normed * normed, axis=-1, keepdims=True))


def mm(a, b):
    return dot(a, b, 1, 0)


def mm_t(a, b):
    return dot(a, b, 1, 1)


def t_mm(a, b):
    return dot(a, b, 0, 0)


def shards(
    hidden_in,
    first_in,
    segment_ids,
    valid_tokens,
    w_query,
    w_key,
    w_value,
    w_first_value,
    w_out,
    w_gate,
    w_up,
    w_down,
    gain_attn,
    gain_mlp,
    out_cotangent,
):
    at = Place()
    bf16, f32 = jnp.bfloat16, jnp.float32
    rows, width = hidden_in.shape
    cols = w_query.shape[1]
    pairs = cols // 128
    hid = w_gate.shape[1]
    beside = lambda *parts: jnp.concatenate(parts, 1)

    inner = [at.slice_of(w) for w in (w_query, w_key, w_value, w_first_value)]
    w_pair = []
    for p in range(pairs):
        low, high = at.quarters(beside(*(w[:, p * 128 : (p + 1) * 128] for w in inner)))
        w_pair.append(at.gathered_direct(beside(low, high)))
    low, high = at.quarters(beside(at.slice_of(w_gate), at.slice_of(w_up)))
    full_gu = at.gathered(beside(low[:, :hid], high[:, :hid], low[:, hid:], high[:, hid:]))
    down_rows, out_rows = hid // at.slots, cols // at.slots
    low, high = at.quarters(jnp.concatenate([at.slice_of(w_down), at.slice_of(w_out)], 0))
    both_do = at.gathered(beside(low, high)).reshape(at.slots, down_rows + out_rows, 2, width)
    stack_rows = lambda a: jnp.concatenate([a[:, :, q].reshape(-1, width) for q in range(2)], 0)
    full_d = stack_rows(both_do[:, :down_rows])
    full_o = stack_rows(both_do[:, down_rows:])

    x_all = at.ordered(hidden_in, moved(hidden_in, 1)).astype(f32)
    first_all = at.ordered(first_in, moved(first_in, 1))
    dy_own = lax.dynamic_slice_in_dim(out_cotangent, at.z * rows, rows, 0)
    dy_all = at.ordered(dy_own, moved(dy_own, 1))
    facts = jnp.stack([segment_ids, valid_tokens])
    facts = at.ordered(facts[None], moved(facts, 1)[None])
    seq_places = jax.vmap(token_places)(facts[:, 0])
    live = lax.dynamic_slice_in_dim(facts[:, 1], at.z * rows, rows, 1).reshape(-1, 1).astype(bf16)
    places = lax.dynamic_slice_in_dim(seq_places, at.z * rows, rows, 1).reshape(-1)
    spots = jnp.arange(segment_ids.shape[0], dtype=jnp.int32)
    unit = at.z // 2
    unit_places = lax.dynamic_index_in_dim(seq_places, unit, 0, keepdims=False)
    unit_live = lax.dynamic_index_in_dim(facts[:, 1], unit, 0, keepdims=False)
    first_key = jnp.where(unit_live == 1, spots - unit_places, spots)[None]
    frequency = jnp.exp(jnp.arange(HD // 2, dtype=f32) * (-2.0 * math.log(10000.0) / HD))
    angles = jnp.concatenate([places, unit_places]).astype(f32)[None, :] * frequency[:, None]
    cos_flat, sin_flat = jnp.cos(angles), jnp.sin(angles)
    n_here = 2 * rows
    cosine = jnp.concatenate([cos_flat] * 4, 0).T
    sine = jnp.concatenate([-sin_flat, sin_flat] * 2, 0).T
    flat = jnp.stack([cos_flat[:, n_here:], sin_flat[:, n_here:]])

    normed_one, inverse_one = rms_parts(x_all)
    h_one = (normed_one * gain_attn).astype(bf16)
    kept = []
    mixed = []
    powers = 0.0
    for p in range(pairs):
        sent, power = project(h_one, first_all, w_pair[p], cosine[:n_here], sine[:n_here])
        powers = powers + jnp.sum(power, 1)
        qkv = exchanged(sent)
        attended, logsum = attend(first_key, qkv)
        kept.append((qkv, attended, logsum))
        mixed.append(exchanged(attended))
    laid = lambda parts: jnp.concatenate(
        [beside(*(parts[p][2 * s + q] for q in range(2) for p in range(pairs))) for s in range(2)], 0
    )
    attn_mixed = laid(mixed) * live

    def both(partial):
        sent = partial.astype(bf16)
        return sent.astype(f32) + moved(sent, 1).astype(f32)

    own_rows = lambda a: lax.dynamic_slice_in_dim(a, at.core * rows, rows, 0)
    other_rows = lambda a: lax.dynamic_slice_in_dim(a, (1 - at.core) * rows, rows, 0)

    residual = x_all + both(mm(attn_mixed, full_o))
    normed_two, inverse_two = rms_parts(residual)
    h_two = (normed_two * gain_mlp).astype(bf16)
    d_hidden = mm_t(dy_all, full_d).astype(bf16).astype(f32)
    gate_up = mm(h_two, full_gu)
    gate, up = gate_up[:, : 2 * hid], gate_up[:, 2 * hid :]
    sigmoid = jax.nn.sigmoid(gate)
    silu = gate * sigmoid
    hidden = (silu * up).astype(bf16)
    d_gate = (d_hidden * up * sigmoid * (1.0 + gate * (1.0 - sigmoid))).astype(bf16)
    d_up = (d_hidden * silu).astype(bf16)
    d_gu = beside(d_gate, d_up)
    d_h2 = both(mm_t(d_gu, full_gu))
    d_res = dy_all.astype(f32) + rms_back(d_h2, normed_two, inverse_two, gain_mlp)
    d_attn = d_res.astype(bf16)
    d_mixed = mm_t(d_attn, full_o).astype(bf16) * live
    incoming = []
    for p in range(pairs):
        cut = lambda s, q: d_mixed[s * rows : (s + 1) * rows, (q * pairs + p) * 128 : (q * pairs + p + 1) * 128]
        incoming.append(exchanged(jnp.stack([cut(s, q) for s in range(2) for q in range(2)])))

    hidden, d_gu, h_two, d_attn = tied((hidden, d_gu, h_two, d_attn), d_mixed)
    ffn = mm(hidden, full_d).astype(bf16)
    ffn = own_rows(ffn).astype(f32) + moved(other_rows(ffn), 1).astype(f32)
    block_out = (own_rows(residual) + ffn).astype(bf16)
    g_gu = t_mm(h_two, d_gu).astype(bf16)
    s_gu = at.scattered(g_gu)
    g_down = t_mm(hidden, dy_all).astype(bf16)
    g_out = t_mm(attn_mixed, d_attn).astype(bf16)
    slotted = lambda g, q, n: g[q * n : (q + 1) * n].reshape(at.slots, n // at.slots, width)
    g_do = jnp.concatenate(
        [jnp.concatenate([slotted(g_down, q, hid), slotted(g_out, q, cols)], 1) for q in range(2)], 2
    ).reshape(-1, 2 * width)
    s_do = at.scattered(g_do)
    low = beside(s_gu[:, :hid], s_gu[:, 2 * hid : 3 * hid])
    high = beside(s_gu[:, hid : 2 * hid], s_gu[:, 3 * hid :])
    all_gu = at.returned(low, high)
    all_do = at.returned(s_do[:, :width], s_do[:, width:]).reshape(at.slots, down_rows + out_rows, width)

    d_h1 = 0.0
    inner_sums = []
    for p in range(pairs):
        qkv, attended, logsum = kept[p]
        back = attend_back(first_key, qkv, attended, incoming[p], logsum, flat, cosine[n_here:], sine[n_here:])
        back = exchanged(back)
        d_inner = jnp.concatenate([beside(back[2 * s], back[2 * s + 1]) for s in range(2)], 0)
        d_first = beside(d_inner[:, 256:384], d_inner[:, 640:768])
        w_inner = beside(w_pair[p][:, :384], w_pair[p][:, 512:896])
        d_h1 = d_h1 + mm_t(d_inner, w_inner)
        g_inner = t_mm(h_one, d_inner).astype(bf16)
        g_first = t_mm(first_all, d_first).astype(bf16)
        g_pair = beside(g_inner[:, :384], g_first[:, :128], g_inner[:, 384:], g_first[:, 128:])
        s_pair = at.scattered_direct(g_pair)
        inner_sums.append(at.returned(s_pair[:, :512], s_pair[:, 512:]))
    d_h1 = d_h1.astype(bf16)
    d_h1 = own_rows(d_h1).astype(f32) + moved(other_rows(d_h1), 1).astype(f32)
    own_normed = own_rows(normed_one)
    grad_input = (own_rows(d_res) + rms_back(d_h1, own_normed, own_rows(inverse_one), gain_attn)).astype(bf16)

    gain_parts = jnp.stack([jnp.sum(d_h1 * own_normed, 0), jnp.sum(own_rows(d_h2 * normed_two), 0)])
    small = jnp.concatenate([gain_parts.reshape(-1), powers[:2], jnp.zeros((126,), f32)])
    small = small.reshape(-1, 128)
    bit = 1
    while bit < at.n_dp:
        small = small + moved(small, bit)
        bit *= 2
    for shift in (1, 2):
        small = small + lax.ppermute(small, "mp", [(i, i ^ shift) for i in range(4)])
    small = small.reshape(-1)
    count = float(rows * at.n_dp * 4 * width)
    inner_out = [
        beside(*(inner_sums[p][:, i * 128 : (i + 1) * 128] for p in range(pairs))).astype(f32) for i in range(4)
    ]
    return (
        block_out,
        grad_input,
        *inner_out,
        all_do[:, down_rows:].reshape(cols, width).astype(f32),
        all_gu[:, :hid].astype(f32),
        all_gu[:, hid:].astype(f32),
        all_do[:, :down_rows].reshape(hid, width).astype(f32),
        small[:width],
        small[width : 2 * width],
        small[2 * width] / count,
        small[2 * width + 1] / count,
    )


def solution(mesh):
    placed = (
        P(("dp", "mp"), None),
        P(("dp", "mp"), None),
        P("dp"),
        P("dp"),
        P(None, "mp"),
        P(None, "mp"),
        P(None, "mp"),
        P(None, "mp"),
        P("mp", None),
        P(None, "mp"),
        P(None, "mp"),
        P("mp", None),
        P(),
        P(),
        P("dp", None),
    )
    return jax.shard_map(
        shards,
        mesh=mesh,
        in_specs=placed,
        out_specs=(
            P(("dp", "mp"), None),
            P(("dp", "mp"), None),
            P(None, "mp"),
            P(None, "mp"),
            P(None, "mp"),
            P(None, "mp"),
            P("mp", None),
            P(None, "mp"),
            P(None, "mp"),
            P("mp", None),
            P(),
            P(),
            P(),
            P(),
        ),
        check_vma=False,
    )
```

```python
import functools
import math

import jax
import jax.numpy as jnp
from jax import lax
from jax.experimental import pallas as pl
from jax.experimental.pallas import tpu as pltpu
from jax.sharding import PartitionSpec as P

HD = 64
norm_eps = 1e-06


def token_places(segment_ids):
    n_tokens = segment_ids.shape[0]
    indices = jnp.arange(n_tokens, dtype=jnp.int32)
    starts_new = jnp.concatenate([jnp.ones((1,), jnp.bool_), segment_ids[1:] != segment_ids[:-1]])
    begins = lax.cummax(jnp.where(starts_new, indices, jnp.zeros_like(indices)), axis=0)
    return indices - begins


QB = 256
VMEM = 48 * 2**20
HINT = pl.CostEstimate(flops=0, bytes_accessed=0, transcendentals=0)


def dot(a, b, ca, cb):
    return lax.dot_general(a, b, (((ca,), (cb,)), ((), ())), preferred_element_type=jnp.float32)


def lane_of(shape):
    return lax.broadcasted_iota(jnp.int32, shape, 1)


def turned(values, cosine, sine):
    near = lane_of(values.shape) % HD < HD // 2
    swapped = jnp.where(near, pltpu.roll(values, 128 - HD // 2, 1), pltpu.roll(values, HD // 2, 1))
    return values * cosine + swapped * sine


def project_kernel(h_ref, first_ref, w_ref, cos_ref, sin_ref, out_ref, power_ref):
    h, first = h_ref[...], first_ref[...]
    cosine, sine = cos_ref[...], sin_ref[...]
    at = pl.program_id(0)

    @pl.when(at == 0)
    def _():
        power_ref[...] = jnp.zeros_like(power_ref)

    for half in range(2):
        base = half * 512
        qkv = dot(h, w_ref[:, base : base + 384], 1, 0)
        raw = dot(first, w_ref[:, base + 384 : base + 512], 1, 0).astype(jnp.bfloat16).astype(jnp.float32)
        out_ref[half, :, 0:128] = turned(qkv[:, 0:128], cosine, sine).astype(jnp.bfloat16) * jnp.bfloat16(0.125)
        out_ref[half, :, 128:256] = turned(qkv[:, 128:256], cosine, sine).astype(jnp.bfloat16)
        blend = (0.5 * qkv[:, 256:384] + 0.5 * raw).astype(jnp.bfloat16)
        out_ref[half, :, 256:384] = blend
        blend = blend.astype(jnp.float32)
        power_ref[0:1, :] += jnp.sum(raw * raw, 0, keepdims=True)
        power_ref[1:2, :] += jnp.sum(blend * blend, 0, keepdims=True)


def project(h, first, weight, cosine, sine):
    n, width = h.shape
    rows = n // 2
    subs = rows // QB
    return pl.pallas_call(
        project_kernel,
        grid=(n // QB,),
        in_specs=[
            pl.BlockSpec((QB, width), lambda i: (i, 0)),
            pl.BlockSpec((QB, width), lambda i: (i, 0)),
            pl.BlockSpec(weight.shape, lambda i: (0, 0)),
            pl.BlockSpec((QB, 128), lambda i: (i, 0)),
            pl.BlockSpec((QB, 128), lambda i: (i, 0)),
        ],
        out_specs=[
            pl.BlockSpec((2, QB, 384), lambda i: (i // subs, i % subs, 0)),
            pl.BlockSpec((8, 128), lambda i: (0, 0)),
        ],
        out_shape=[
            jax.ShapeDtypeStruct((4, rows, 384), jnp.bfloat16),
            jax.ShapeDtypeStruct((8, 128), jnp.float32),
        ],
        compiler_params=pltpu.CompilerParams(vmem_limit_bytes=VMEM),
        cost_estimate=HINT,
    )(h, first, weight, cosine, sine)


def causal(scores, start, q_pos, i, rows, last):
    k_pos = i * rows + lax.broadcasted_iota(jnp.int32, scores.shape, 0)
    keep = k_pos >= start
    if last:
        keep = keep & (k_pos <= q_pos)
    return jnp.where(keep, scores, -1e30)


def attend_kernel(start_ref, q_ref, k_ref, v_ref, o_ref, lse_ref, *, pieces, rows):
    for j in range(pieces):
        for sub in range(rows // QB):
            first = j * rows + sub * QB
            q_pair = q_ref[j, sub * QB : (sub + 1) * QB, :]
            start = start_ref[0:1, first : first + QB]
            q_pos = first + lane_of((1, QB))
            outs = []
            for head in range(2):
                mine = lane_of(q_pair.shape) // HD == head
                qm = jnp.where(mine, q_pair, jnp.zeros_like(q_pair))
                blocks = []
                for i in range(j + 1):
                    n = rows if i < j else (sub + 1) * QB
                    s = dot(k_ref[i, :n, :], qm, 1, 1)
                    blocks.append((i, n, causal(s, start, q_pos, i, rows, i == j)))
                peak = functools.reduce(jnp.maximum, [jnp.max(b[2], 0, keepdims=True) for b in blocks])
                total = 0.0
                acc = 0.0
                for i, n, s in blocks:
                    p = jnp.exp(s - peak)
                    total = total + jnp.sum(p, 0, keepdims=True)
                    acc = acc + dot(v_ref[i, :n, :], p.astype(jnp.bfloat16), 0, 0)
                outs.append((acc / total)[head * HD : (head + 1) * HD])
                lse_ref[head : head + 1, first : first + QB] = peak + jnp.log(total)
            o_ref[j, sub * QB : (sub + 1) * QB, :] = jnp.transpose(jnp.concatenate(outs, 0)).astype(o_ref.dtype)


def column(pieces, rows, at):
    return pl.BlockSpec((pieces, rows, 128), lambda _: (0, 0, at))


def whole(shape):
    return pl.BlockSpec(shape, lambda _: (0,) * len(shape))


def attend(start, qkv):
    pieces, rows, _ = qkv.shape
    n = pieces * rows
    return pl.pallas_call(
        functools.partial(attend_kernel, pieces=pieces, rows=rows),
        grid=(1,),
        in_specs=[whole((1, n))] + [column(pieces, rows, i) for i in range(3)],
        out_specs=[whole((pieces, rows, 128)), whole((2, n))],
        out_shape=[
            jax.ShapeDtypeStruct((pieces, rows, 128), jnp.bfloat16),
            jax.ShapeDtypeStruct((2, n), jnp.float32),
        ],
        compiler_params=pltpu.CompilerParams(vmem_limit_bytes=VMEM),
        cost_estimate=HINT,
    )(start, qkv, qkv, qkv)


def back_kernel(
    start_ref, q_ref, k_ref, v_ref, o_ref, g_ref, lse_ref, flat_ref, cos_ref, sin_ref, d_ref, acc_k, acc_v, *, pieces, rows
):
    acc_k[...] = jnp.zeros_like(acc_k)
    acc_v[...] = jnp.zeros_like(acc_v)
    low = HD // 2
    for j in range(pieces):
        for sub in range(rows // QB):
            first = j * rows + sub * QB
            here = slice(sub * QB, (sub + 1) * QB)
            q_pair = q_ref[j, here, :]
            g_pair = g_ref[j, here, :]
            start = start_ref[0:1, first : first + QB]
            q_pos = first + lane_of((1, QB))
            inner = jnp.transpose(o_ref[j, here, :].astype(jnp.float32) * g_pair.astype(jnp.float32))
            cosine = flat_ref[0, :, first : first + QB]
            sine = flat_ref[1, :, first : first + QB]
            outs = []
            for head in range(2):
                mine = lane_of(q_pair.shape) // HD == head
                qm = jnp.where(mine, q_pair, jnp.zeros_like(q_pair))
                gm = jnp.where(mine, g_pair, jnp.zeros_like(g_pair))
                delta = jnp.sum(inner[head * HD : (head + 1) * HD], 0, keepdims=True)
                lse = lse_ref[head : head + 1, first : first + QB]
                acc = 0.0
                for i in range(j + 1):
                    n = rows if i < j else (sub + 1) * QB
                    k_blk = k_ref[i, :n, :]
                    s = causal(dot(k_blk, qm, 1, 1), start, q_pos, i, rows, i == j)
                    p = jnp.exp(s - lse)
                    dp = dot(v_ref[i, :n, :], gm, 1, 1)
                    ds = (p * (dp - delta)).astype(jnp.bfloat16)
                    acc_v[i, :n, :] += dot(p.astype(jnp.bfloat16), gm, 1, 0)
                    acc_k[i, :n, :] += dot(ds, qm, 1, 0)
                    acc = acc + dot(k_blk, ds, 0, 0)
                near = acc[head * HD : head * HD + low] * 0.125
                far = acc[head * HD + low : (head + 1) * HD] * 0.125
                outs += [near * cosine + far * sine, far * cosine - near * sine]
            d_ref[j, here, 0:128] = jnp.transpose(jnp.concatenate(outs, 0)).astype(d_ref.dtype)
    for j in range(pieces):
        here = slice(j * rows, (j + 1) * rows)
        d_ref[j, :, 128:256] = turned(acc_k[j], cos_ref[here, :], -sin_ref[here, :]).astype(d_ref.dtype)
        d_ref[j, :, 256:384] = acc_v[j].astype(d_ref.dtype) * jnp.bfloat16(0.5)


def attend_back(start, qkv, o, g, lse, flat, cosine, sine):
    pieces, rows, _ = qkv.shape
    n = pieces * rows
    one = whole((pieces, rows, 128))
    return pl.pallas_call(
        functools.partial(back_kernel, pieces=pieces, rows=rows),
        grid=(1,),
        in_specs=[whole((1, n))]
        + [column(pieces, rows, i) for i in range(3)]
        + [one, one, whole((2, n)), whole(flat.shape), whole((n, 128)), whole((n, 128))],
        out_specs=whole((pieces, rows, 384)),
        scratch_shapes=[pltpu.VMEM((pieces, rows, 128), jnp.float32)] * 2,
        out_shape=jax.ShapeDtypeStruct((pieces, rows, 384), jnp.bfloat16),
        compiler_params=pltpu.CompilerParams(vmem_limit_bytes=VMEM),
        cost_estimate=HINT,
    )(start, qkv, qkv, qkv, o, g, lse, flat, cosine, sine)


def rows_spec(block, width):
    return pl.BlockSpec((block, width), lambda i, *_: (i, 0))


def fixed(shape):
    return pl.BlockSpec(shape, lambda i, *_: (0,) * len(shape))


def mix_kernel(*refs, pairs, block):
    parts, (live_ref, w_ref, mixed_ref, out_ref) = refs[:pairs], refs[pairs:]
    live = live_ref[...]
    for q in range(2):
        for p in range(pairs):
            at = (q * pairs + p) * 128
            mixed_ref[:, at : at + 128] = parts[p][q] * live
    out_ref[...] = dot(mixed_ref[...], w_ref[...], 1, 0).astype(out_ref.dtype)


def mix(parts, live, weight):
    pairs = len(parts)
    rows = parts[0].shape[1]
    inner, width = weight.shape
    block = rows
    return pl.pallas_call(
        functools.partial(mix_kernel, pairs=pairs, block=block),
        grid=(2,),
        in_specs=[pl.BlockSpec((2, block, 128), lambda i: (i, 0, 0))] * pairs
        + [rows_spec(block, 1), fixed(weight.shape)],
        out_specs=[rows_spec(block, inner), rows_spec(block, width)],
        out_shape=[
            jax.ShapeDtypeStruct((2 * rows, inner), jnp.bfloat16),
            jax.ShapeDtypeStruct((2 * rows, width), jnp.bfloat16),
        ],
        compiler_params=pltpu.CompilerParams(vmem_limit_bytes=VMEM),
        cost_estimate=HINT,
    )(*parts, live, weight)


def feed_kernel(x_ref, mine_ref, other_ref, gain_ref, dy_ref, *refs):
    weights, (down_ref, res_ref, h_ref, hid_ref, d_ref, out_ref) = refs[:2], refs[2:]
    f32 = jnp.float32
    pad = down_ref.shape[0] // 2
    res = x_ref[...].astype(f32) + (mine_ref[...].astype(f32) + other_ref[...].astype(f32))
    res_ref[...] = res
    inverse = lax.rsqrt(jnp.mean(res * res, axis=-1, keepdims=True) + norm_eps)
    h = (res * inverse * gain_ref[...]).astype(jnp.bfloat16)
    h_ref[...] = h
    dy = dy_ref[...]
    for q in range(2):
        for at in range(0, pad, 256):
            near = slice(q * 2 * pad + at, q * 2 * pad + at + 256)
            far = slice(q * 2 * pad + pad + at, q * 2 * pad + pad + at + 256)
            here = slice(q * pad + at, q * pad + at + 256)
            gate = dot(h, weights[q][:, at : at + 256], 1, 0)
            up = dot(h, weights[q][:, pad + at : pad + at + 256], 1, 0)
            d_hid = dot(dy, down_ref[here, :], 1, 1).astype(jnp.bfloat16).astype(f32)
            sig = 1.0 / (1.0 + jnp.exp(-gate))
            silu = gate * sig
            hid_ref[:, here] = (silu * up).astype(jnp.bfloat16)
            d_ref[:, near] = (d_hid * up * (sig * (1.0 + gate * (1.0 - sig)))).astype(jnp.bfloat16)
            d_ref[:, far] = (d_hid * silu).astype(jnp.bfloat16)
    total = dot(d_ref[:, : 2 * pad], weights[0][:, : 2 * pad], 1, 1)
    total = total + dot(d_ref[:, 2 * pad :], weights[1][:, : 2 * pad], 1, 1)
    out_ref[...] = total.astype(jnp.bfloat16)


def feed(x, mine, other, gain, dy, weights, down):
    n, width = x.shape
    pad = down.shape[0] // 2
    span = weights.shape[1] // 2
    block = n // 4
    tokens = rows_spec(block, width)
    bf16 = jnp.bfloat16
    quarter = lambda q: pl.BlockSpec((width, span), lambda i: (0, q))
    return pl.pallas_call(
        feed_kernel,
        grid=(n // block,),
        in_specs=[tokens, tokens, tokens, fixed((1, width)), tokens, quarter(0), quarter(1), fixed(down.shape)],
        out_specs=[tokens, tokens, rows_spec(block, 2 * pad), rows_spec(block, 4 * pad), tokens],
        out_shape=[
            jax.ShapeDtypeStruct((n, width), jnp.float32),
            jax.ShapeDtypeStruct((n, width), bf16),
            jax.ShapeDtypeStruct((n, 2 * pad), bf16),
            jax.ShapeDtypeStruct((n, 4 * pad), bf16),
            jax.ShapeDtypeStruct((n, width), bf16),
        ],
        compiler_params=pltpu.CompilerParams(vmem_limit_bytes=VMEM),
        cost_estimate=HINT,
    )(x, mine, other, gain, dy, weights, weights, down)


def turn_kernel(core_ref, res_ref, mine_ref, other_ref, dy_ref, gain_ref, w_ref, live_ref, dres_ref, dattn_ref, gains_ref, *outs):
    f32 = jnp.float32
    pairs = len(outs)
    res = res_ref[...]
    inverse = lax.rsqrt(jnp.mean(res * res, axis=-1, keepdims=True) + norm_eps)
    normed = res * inverse
    grad = mine_ref[...].astype(f32) + other_ref[...].astype(f32)
    scaled = grad * gain_ref[...]
    d_res = dy_ref[...].astype(f32) + inverse * (scaled - normed * jnp.mean(scaled * normed, axis=-1, keepdims=True))
    dres_ref[...] = d_res
    d_attn = d_res.astype(jnp.bfloat16)
    dattn_ref[...] = d_attn
    mixed = dot(d_attn, w_ref[...], 1, 1).astype(jnp.bfloat16) * live_ref[...]
    for q in range(2):
        for p in range(pairs):
            at = (q * pairs + p) * 128
            outs[p][q] = mixed[:, at : at + 128]
    at = pl.program_id(0)

    @pl.when(at == 0)
    def _():
        gains_ref[...] = jnp.zeros_like(gains_ref)

    @pl.when(at // (pl.num_programs(0) // 2) == core_ref[0])
    def _():
        gains_ref[0:1, :] += jnp.sum(grad * normed, 0, keepdims=True)


def turn(core, res, mine, other, dy, gain, weight, live):
    n, width = res.shape
    inner = weight.shape[0]
    pairs = inner // 256
    rows = n // 2
    block = rows // 2
    subs = rows // block
    tokens = rows_spec(block, width)
    packed = pl.BlockSpec((2, block, 128), lambda i, *_: (i // subs, i % subs, 0))
    return pl.pallas_call(
        turn_kernel,
        grid_spec=pltpu.PrefetchScalarGridSpec(
            num_scalar_prefetch=1,
            grid=(n // block,),
            in_specs=[tokens] * 4 + [fixed((1, width)), fixed(weight.shape), rows_spec(block, 1)],
            out_specs=[tokens, tokens, fixed((8, width))] + [packed] * pairs,
        ),
        out_shape=[
            jax.ShapeDtypeStruct((n, width), jnp.float32),
            jax.ShapeDtypeStruct((n, width), jnp.bfloat16),
            jax.ShapeDtypeStruct((8, width), jnp.float32),
        ]
        + [jax.ShapeDtypeStruct((4, rows, 128), jnp.bfloat16)] * pairs,
        compiler_params=pltpu.CompilerParams(vmem_limit_bytes=VMEM),
        cost_estimate=HINT,
    )(core, res, mine, other, dy, gain, weight, live)


def weigh_kernel(a_ref, b_ref, out_ref):
    out_ref[...] = dot(a_ref[...], b_ref[...], 0, 0).astype(out_ref.dtype)


def weigh(a, b):
    n, left = a.shape
    right = b.shape[1]
    wide = next(w for w in (1024, 768, 512, 256, right) if right % w == 0)
    return pl.pallas_call(
        weigh_kernel,
        grid=(right // wide,),
        in_specs=[pl.BlockSpec((n, left), lambda i: (0, 0)), pl.BlockSpec((n, wide), lambda i: (0, i))],
        out_specs=pl.BlockSpec((left, wide), lambda i: (0, i)),
        out_shape=jax.ShapeDtypeStruct((left, right), jnp.bfloat16),
        compiler_params=pltpu.CompilerParams(vmem_limit_bytes=VMEM),
        cost_estimate=HINT,
    )(a, b)


def slices_kernel(slot_ref, *refs, pairs):
    ins, outs = refs[:4], refs[4:]
    for p in range(pairs):
        for i in range(4):
            outs[p][:, i * 128 : (i + 1) * 128] = ins[i][:, p * 128 : (p + 1) * 128]


def inner_slices(slot, weights, slots):
    width, cols = weights[0].shape
    rows, pairs = width // slots, cols // 128
    return pl.pallas_call(
        functools.partial(slices_kernel, pairs=pairs),
        grid_spec=pltpu.PrefetchScalarGridSpec(
            num_scalar_prefetch=1,
            grid=(1,),
            in_specs=[pl.BlockSpec((rows, cols), lambda i, slot: (slot[0], 0))] * 4,
            out_specs=[pl.BlockSpec((rows, 512), lambda i, slot: (0, 0))] * pairs,
        ),
        out_shape=[jax.ShapeDtypeStruct((rows, 512), jnp.bfloat16)] * pairs,
        compiler_params=pltpu.CompilerParams(vmem_limit_bytes=VMEM),
        cost_estimate=HINT,
    )(slot, *weights)


def spread_gu_kernel(sum_ref, gate_ref, up_ref):
    hid, pad = gate_ref.shape[1], sum_ref.shape[1] // 2
    gate_ref[...] = sum_ref[:, :hid].astype(jnp.float32)
    up_ref[...] = sum_ref[:, pad : pad + hid].astype(jnp.float32)


def spread_gu(total, pad, hid):
    n = total.shape[0]
    block = n // 4
    return pl.pallas_call(
        spread_gu_kernel,
        grid=(4,),
        in_specs=[rows_spec(block, 2 * pad)],
        out_specs=[rows_spec(block, hid)] * 2,
        out_shape=[jax.ShapeDtypeStruct((n, hid), jnp.float32)] * 2,
        compiler_params=pltpu.CompilerParams(vmem_limit_bytes=VMEM),
        cost_estimate=HINT,
    )(total)


def spread_do_kernel(sum_ref, down_ref, out_ref):
    n_down, n_out = down_ref.shape[0], out_ref.shape[0]
    down_ref[...] = sum_ref[:n_down, :].astype(jnp.float32)
    out_ref[...] = sum_ref[n_down : n_down + n_out, :].astype(jnp.float32)


def spread_do(total, slots, down_rows, out_rows, width):
    rows = total.shape[0] // slots
    shapes = [(down_rows, width), (out_rows, width)]
    return pl.pallas_call(
        spread_do_kernel,
        grid=(slots,),
        in_specs=[rows_spec(rows, width)],
        out_specs=[rows_spec(*s) for s in shapes],
        out_shape=[jax.ShapeDtypeStruct((s[0] * slots, s[1]), jnp.float32) for s in shapes],
        compiler_params=pltpu.CompilerParams(vmem_limit_bytes=VMEM),
        cost_estimate=HINT,
    )(total)


def inner_kernel(*refs):
    ins, outs = refs[:-4], refs[-4:]
    for p, ref in enumerate(ins):
        for i in range(4):
            outs[i][:, p * 128 : (p + 1) * 128] = ref[:, i * 128 : (i + 1) * 128].astype(jnp.float32)


def inner_spread(parts):
    n = parts[0][0].shape[0]
    block = n // 2
    cols = 128 * len(parts)
    at = lambda col: pl.BlockSpec((block, 512), lambda i: (i, col))
    return pl.pallas_call(
        inner_kernel,
        grid=(2,),
        in_specs=[at(col) for _, col in parts],
        out_specs=[rows_spec(block, cols)] * 4,
        out_shape=[jax.ShapeDtypeStruct((n, cols), jnp.float32)] * 4,
        compiler_params=pltpu.CompilerParams(vmem_limit_bytes=VMEM),
        cost_estimate=HINT,
    )(*(a for a, _ in parts))


def multiply_kernel(a_ref, b_ref, out_ref):
    out_ref[...] = dot(a_ref[...], b_ref[...], 1, 0).astype(out_ref.dtype)


def multiply(a, b):
    n, width = a.shape[0], b.shape[1]
    block = n // 4
    return pl.pallas_call(
        multiply_kernel,
        grid=(4,),
        in_specs=[rows_spec(block, a.shape[1]), fixed(b.shape)],
        out_specs=rows_spec(block, width),
        out_shape=jax.ShapeDtypeStruct((n, width), jnp.bfloat16),
        compiler_params=pltpu.CompilerParams(vmem_limit_bytes=VMEM),
        cost_estimate=HINT,
    )(a, b)


def moved(values, bit):
    return lax.ppermute(values, "dp", [(i, i ^ bit) for i in range(lax.axis_size("dp"))])


def cross_pairs(n_dp):
    pairs = []
    for d in range(n_dp):
        for z in range(4):
            pairs.append((d * 4 + z, d * 4 + (z ^ 1) if z // 2 == d % 2 else (d ^ 1) * 4 + (z ^ 2)))
    return pairs


def side_pairs(n_dp):
    return [(d * 4 + z, d * 4 + (z ^ 1)) for d in range(n_dp) for z in range(4) if z // 2 != d % 2]


def tied(values, *others):
    return lax.optimization_barrier((values, others))[0]


class Place:
    def __init__(self):
        self.n_dp = lax.axis_size("dp")
        self.slots = self.n_dp // 2
        self.d = lax.axis_index("dp")
        self.z = lax.axis_index("mp")
        self.core = self.d % 2
        self.slot = self.d // 2
        self.own = (self.z // 2) == self.core
        self.even = (self.z % 2) == 0
        self.sides = [[2 * i + c for i in range(self.slots)] for c in range(2)]

    def cross(self, values):
        return lax.ppermute(values, ("dp", "mp"), cross_pairs(self.n_dp))

    def side(self, values):
        return lax.ppermute(values, ("dp", "mp"), side_pairs(self.n_dp))

    def ordered(self, mine, other):
        return jnp.where(self.core == 0, jnp.concatenate([mine, other], 0), jnp.concatenate([other, mine], 0))

    def slice_of(self, weight):
        rows = weight.shape[0] // self.slots
        return lax.dynamic_slice_in_dim(weight, self.slot * rows, rows, 0)

    def quarters(self, part, got):
        far = self.side(got)
        first = jnp.where(self.own, part, got)
        second = jnp.where(self.own, got, far)
        return jnp.where(self.even, first, second), jnp.where(self.even, second, first)

    def gathered(self, part):
        return lax.all_gather(part, "dp", axis=0, tiled=True, axis_index_groups=self.sides)

    def gathered_direct(self, part):
        every = jnp.concatenate([part] * self.slots, 0)
        return lax.all_to_all(every, "dp", 0, 0, tiled=True, axis_index_groups=self.sides)

    def gathered_steps(self, part):
        if self.slots != 4:
            return self.gathered(part)
        rows = part.shape[0]
        every = jnp.zeros((4 * rows, part.shape[1]), part.dtype)
        for k, piece in enumerate((part, moved(part, 2), moved(part, 4), moved(part, 6))):
            every = lax.dynamic_update_slice_in_dim(every, piece, (self.slot ^ k) * rows, 0)
        return every

    def gathered_pairs(self, part):
        return lax.all_to_all(jnp.concatenate([part] * self.n_dp, 0), "dp", 0, 0, tiled=True)

    def scattered(self, values):
        return lax.psum_scatter(values, "dp", scatter_dimension=0, tiled=True, axis_index_groups=self.sides)

    def pieces(self, values):
        if self.slots != 4:
            return [self.scattered(values)]
        rows = values.shape[0] // 4
        pick = lambda k: lax.dynamic_slice_in_dim(values, (self.slot ^ k) * rows, rows, 0)
        return [pick(0), moved(pick(1), 2), moved(pick(2), 4), moved(pick(3), 6)]

    def added(self, parts):
        return sum(p.astype(jnp.float32) for p in parts).astype(jnp.bfloat16)

    def swapped(self, values):
        every = lax.all_to_all(values, "dp", 0, 0, tiled=True, axis_index_groups=self.sides)
        return list(every.reshape((self.slots, -1) + every.shape[1:]))

    def bring(self, low, high):
        first = jnp.where(self.even, low, high)
        second = jnp.where(self.even, high, low)
        return first, second, self.side(second)

    def bring_across(self, first, second, far):
        total = (first.astype(jnp.float32) + far.astype(jnp.float32)).astype(jnp.bfloat16)
        return self.cross(jnp.where(self.own, second, total))

    def bring_home(self, first, got):
        f32, bf16 = jnp.float32, jnp.bfloat16
        part = jnp.where(self.own, (first.astype(f32) + got.astype(f32)).astype(bf16), got)
        half = first.shape[0] // 2
        cut = lambda which: lax.dynamic_slice_in_dim(part, which * half, half, 0)
        return (cut(self.core).astype(f32) + moved(cut(1 - self.core), 1).astype(f32)).astype(bf16)


def exchanged(values):
    return lax.all_to_all(values, "mp", 0, 0, tiled=True)


def rms_parts(values):
    inverse = lax.rsqrt(jnp.mean(values * values, axis=-1, keepdims=True) + norm_eps)
    return (values * inverse, inverse)


def rms_back(grad_rows, normed, inverse, gain_vec):
    grad_normed = grad_rows * gain_vec
    return inverse * (grad_normed - normed * jnp.mean(grad_normed * normed, axis=-1, keepdims=True))


def mm(a, b):
    return dot(a, b, 1, 0)


def mm_t(a, b):
    return dot(a, b, 1, 1)


def t_mm(a, b):
    return dot(a, b, 0, 0)


def shards(
    hidden_in,
    first_in,
    segment_ids,
    valid_tokens,
    w_query,
    w_key,
    w_value,
    w_first_value,
    w_out,
    w_gate,
    w_up,
    w_down,
    gain_attn,
    gain_mlp,
    out_cotangent,
):
    at = Place()
    bf16, f32 = jnp.bfloat16, jnp.float32
    rows, width = hidden_in.shape
    cols = w_query.shape[1]
    pairs = cols // 128
    hid = w_gate.shape[1]
    pad = -(-hid // 256) * 256
    beside = lambda *parts: jnp.concatenate(parts, 1)

    slot = at.slot.reshape(1).astype(jnp.int32)
    parts = inner_slices(slot, (w_query, w_key, w_value, w_first_value), at.slots)
    down_rows, out_rows = hid // at.slots, cols // at.slots
    tall = width // at.slots
    got_pair = []
    before = ()
    for part in parts:
        part = tied(part, before)
        before = at.cross(part)
        got_pair.append((part, before))
    wider = jnp.zeros((tall, pad - hid), bf16)
    outer = jnp.concatenate(
        [at.slice_of(w_down), at.slice_of(w_out), jnp.zeros((tall - down_rows - out_rows, width), bf16)], 0
    )
    part = tied(beside(at.slice_of(w_gate), wider, at.slice_of(w_up), wider, outer), before)
    got_feed = (part, at.cross(part))
    near = [beside(*at.quarters(part, got)) for part, got in got_pair]
    w_pair = [at.gathered_direct(near[0])]

    x_all = at.ordered(*tied((hidden_in, moved(hidden_in, 1)), near[0]))
    first_all = at.ordered(*tied((first_in, moved(first_in, 1)), near[0]))
    facts = jnp.stack([segment_ids, valid_tokens])
    facts = tied(at.ordered(facts[None], moved(facts, 1)[None]), near[0])
    seq_places = jax.vmap(token_places)(facts[:, 0])
    live = lax.dynamic_slice_in_dim(facts[:, 1], at.z * rows, rows, 1).reshape(-1, 1).astype(bf16)
    places = lax.dynamic_slice_in_dim(seq_places, at.z * rows, rows, 1).reshape(-1)
    spots = jnp.arange(segment_ids.shape[0], dtype=jnp.int32)
    unit = at.z // 2
    unit_places = lax.dynamic_index_in_dim(seq_places, unit, 0, keepdims=False)
    unit_live = lax.dynamic_index_in_dim(facts[:, 1], unit, 0, keepdims=False)
    first_key = jnp.where(unit_live == 1, spots - unit_places, spots)[None]
    frequency = jnp.exp(jnp.arange(HD // 2, dtype=f32) * (-2.0 * math.log(10000.0) / HD))
    angles = jnp.concatenate([places, unit_places]).astype(f32)[None, :] * frequency[:, None]
    cos_flat, sin_flat = jnp.cos(angles), jnp.sin(angles)
    n_here = 2 * rows
    cosine = jnp.concatenate([cos_flat] * 4, 0).T
    sine = jnp.concatenate([-sin_flat, sin_flat] * 2, 0).T
    flat = jnp.stack([cos_flat[:, n_here:], sin_flat[:, n_here:]])

    normed_one, inverse_one = rms_parts(x_all.astype(f32))
    h_one = (normed_one * gain_attn).astype(bf16)
    kept = []
    mixed = []
    powers = 0.0
    sends = []
    for p in range(pairs):
        if p == 1:
            part, got = got_feed
            feed_part = tied(beside(*at.quarters(part, got)), (sends, first_key, flat, cosine, sine))
        if p:
            w_pair.append(at.gathered_steps(tied(near[p], feed_part)))
        sent, power = project(h_one, first_all, w_pair[p], cosine[:n_here], sine[:n_here])
        powers = powers + jnp.sum(power, 1)
        sends.append(sent)
    full = at.gathered(feed_part)
    span = 2 * pad + width
    both_do = full.reshape(at.slots, tall, 2 * span)
    lanes = lambda q: slice(q * span + 2 * pad, (q + 1) * span)
    nothing = jnp.zeros((pad - hid, width), bf16)
    full_d = jnp.concatenate(
        [a for q in range(2) for a in (both_do[:, :down_rows, lanes(q)].reshape(hid, width), nothing)], 0
    )
    full_o = jnp.concatenate(
        [both_do[:, down_rows : down_rows + out_rows, lanes(q)].reshape(cols, width) for q in range(2)], 0
    )

    for p in range(pairs):
        qkv = exchanged(sends[p])
        attended, logsum = attend(first_key, qkv)
        kept.append((qkv, attended, logsum))
        mixed.append(exchanged(attended))
    dy_own = tied(lax.dynamic_slice_in_dim(out_cotangent, at.z * rows, rows, 0), sends)
    dy_all = at.ordered(dy_own, moved(dy_own, 1))

    own_rows = lambda a: lax.dynamic_slice_in_dim(a, at.core * rows, rows, 0)
    other_rows = lambda a: lax.dynamic_slice_in_dim(a, (1 - at.core) * rows, rows, 0)

    attn_mixed, out_part = mix(mixed, live, full_o)
    residual, h_two, hidden, d_gu, d_part = feed(
        x_all, out_part, moved(out_part, 1), gain_mlp[None], dy_all, full, full_d
    )
    d_other = moved(d_part, 1)
    g_gu = weigh(h_two, d_gu)
    s_gu = at.scattered(g_gu)
    d_res, d_attn, gains, *sends = turn(
        at.core.reshape(1), tied(residual, g_gu), d_part, d_other, dy_all, gain_mlp[None], full_o, live
    )
    incoming = [exchanged(sent) for sent in sends]

    g_down = weigh(tied(hidden, sends), dy_all)
    g_out = weigh(attn_mixed, d_attn)
    blank = jnp.zeros((at.slots, tall - down_rows - out_rows, width), bf16)
    slotted = lambda g, first, n: g[first : first + n].reshape(at.slots, n // at.slots, width)
    g_do = jnp.concatenate(
        [
            jnp.concatenate([slotted(g_down, q * pad, hid), slotted(g_out, q * cols, cols), blank], 1)
            for q in range(2)
        ],
        2,
    ).reshape(-1, 2 * width)
    s_do = at.scattered(g_do)
    backs = []
    key = tied(first_key, (g_down, g_out))
    for p in range(pairs):
        qkv, attended, logsum = kept[p]
        back = attend_back(key, qkv, attended, incoming[p], logsum, flat, cosine[n_here:], sine[n_here:])
        backs.append(exchanged(back))
        if p == 0:
            ffn = multiply(tied(hidden, back), full_d)
            tied_gu = tied(s_gu, back)
            first_gu, second_gu, far_gu = at.bring(tied_gu[:, : 2 * pad], tied_gu[:, 2 * pad :])
            key = tied(key, (far_gu, ffn))
    got_gu = at.bring_across(first_gu, second_gu, far_gu)
    near_gu = at.bring_home(first_gu, got_gu)
    ffn = own_rows(ffn).astype(f32) + moved(other_rows(ffn), 1).astype(f32)
    block_out = (own_rows(residual) + ffn).astype(bf16)

    d_h1 = 0.0
    parts = []
    sent_pair = ()
    for p in range(pairs):
        back = tied(backs[p], (block_out, got_gu, sent_pair))
        d_inner = jnp.concatenate([beside(back[2 * s], back[2 * s + 1]) for s in range(2)], 0)
        d_first = beside(d_inner[:, 256:384], d_inner[:, 640:768])
        w_inner = beside(w_pair[p][:, :384], w_pair[p][:, 512:896])
        d_h1 = d_h1 + mm_t(d_inner, w_inner)
        g_inner = weigh(h_one, d_inner)
        g_first = weigh(first_all, d_first)
        g_pair = beside(g_inner[:, :384], g_first[:, :128], g_inner[:, 384:], g_first[:, 128:])
        parts.append(at.swapped(g_pair) if p else at.pieces(g_pair))
        sent_pair = g_pair
    sum_gu = lax.all_gather(near_gu, "dp", axis=0, tiled=True)
    most = at.added(tied(parts[0], backs))
    first, second, far = at.bring(
        *(beside(s_do[:, q * width : (q + 1) * width], most[:, q * 512 : (q + 1) * 512]) for q in range(2))
    )
    got = at.bring_across(first, second, tied(far, parts))
    late = [at.added(part) for part in parts[1:]]
    late = [at.bring(part[:, :512], part[:, 512:]) for part in late]
    most = at.bring_home(first, tied(got, (late, sum_gu)))
    sum_do = lax.all_gather(most, "dp", axis=0, tiled=True)
    late = [at.bring_home(one, at.bring_across(one, two, three)) for one, two, three in late]
    inner_sums = [(sum_do, width // 512)] + [(at.gathered_pairs(part), 0) for part in late]
    grad_gate, grad_up = spread_gu(sum_gu, pad, hid)
    if down_rows % 16 == 0:
        grad_down, grad_out = spread_do(sum_do, at.slots, down_rows, out_rows, width)
    else:
        all_do = sum_do[:, :width].reshape(at.slots, tall, width)
        grad_down = all_do[:, :down_rows].reshape(hid, width).astype(f32)
        grad_out = all_do[:, down_rows : down_rows + out_rows].reshape(cols, width).astype(f32)
    d_h1 = d_h1.astype(bf16)
    d_h1 = own_rows(d_h1).astype(f32) + moved(other_rows(d_h1), 1).astype(f32)
    own_normed = own_rows(normed_one)
    grad_input = (own_rows(d_res) + rms_back(d_h1, own_normed, own_rows(inverse_one), gain_attn)).astype(bf16)

    gain_parts = jnp.stack([jnp.sum(d_h1 * own_normed, 0), gains[0]])
    small = jnp.concatenate([gain_parts.reshape(-1), powers[:2], jnp.zeros((126,), f32)])
    small = small.reshape(-1, 128)
    small = jnp.pad(small, ((0, -small.shape[0] % 8), (0, 0)))
    for axis, size in (("dp", at.n_dp), ("mp", 4)):
        every = lax.all_to_all(jnp.concatenate([small] * size, 0), axis, 0, 0, tiled=True)
        small = jnp.sum(every.reshape((size,) + small.shape), 0)
    small = small.reshape(-1)
    count = float(rows * at.n_dp * 4 * width)
    return (
        block_out,
        grad_input,
        *inner_spread(inner_sums),
        grad_out,
        grad_gate,
        grad_up,
        grad_down,
        small[:width],
        small[width : 2 * width],
        small[2 * width] / count,
        small[2 * width + 1] / count,
    )


def solution(mesh):
    placed = (
        P(("dp", "mp"), None),
        P(("dp", "mp"), None),
        P("dp"),
        P("dp"),
        P(None, "mp"),
        P(None, "mp"),
        P(None, "mp"),
        P(None, "mp"),
        P("mp", None),
        P(None, "mp"),
        P(None, "mp"),
        P("mp", None),
        P(),
        P(),
        P("dp", None),
    )
    return jax.shard_map(
        shards,
        mesh=mesh,
        in_specs=placed,
        out_specs=(
            P(("dp", "mp"), None),
            P(("dp", "mp"), None),
            P(None, "mp"),
            P(None, "mp"),
            P(None, "mp"),
            P(None, "mp"),
            P("mp", None),
            P(None, "mp"),
            P(None, "mp"),
            P("mp", None),
            P(),
            P(),
            P(),
            P(),
        ),
        check_vma=False,
    )
```

```python
import functools
import math

import jax
import jax.numpy as jnp
from jax import lax
from jax.experimental import pallas as pl
from jax.experimental.pallas import tpu as pltpu
from jax.sharding import PartitionSpec as P

HD = 64
norm_eps = 1e-06


def token_places(segment_ids):
    n_tokens = segment_ids.shape[0]
    indices = jnp.arange(n_tokens, dtype=jnp.int32)
    starts_new = jnp.concatenate([jnp.ones((1,), jnp.bool_), segment_ids[1:] != segment_ids[:-1]])
    begins = lax.cummax(jnp.where(starts_new, indices, jnp.zeros_like(indices)), axis=0)
    return indices - begins


QB = 256
VMEM = 48 * 2**20
HINT = pl.CostEstimate(flops=0, bytes_accessed=0, transcendentals=0)


def dot(a, b, ca, cb):
    return lax.dot_general(a, b, (((ca,), (cb,)), ((), ())), preferred_element_type=jnp.float32)


def lane_of(shape):
    return lax.broadcasted_iota(jnp.int32, shape, 1)


def turned(values, cosine, sine):
    near = lane_of(values.shape) % HD < HD // 2
    swapped = jnp.where(near, pltpu.roll(values, 128 - HD // 2, 1), pltpu.roll(values, HD // 2, 1))
    return values * cosine + swapped * sine


def project_kernel(h_ref, first_ref, w_ref, cos_ref, sin_ref, out_ref, power_ref):
    h, first = h_ref[...], first_ref[...]
    cosine, sine = cos_ref[...], sin_ref[...]
    at = pl.program_id(0)

    @pl.when(at == 0)
    def _():
        power_ref[...] = jnp.zeros_like(power_ref)

    for half in range(2):
        base = half * 512
        qkv = dot(h, w_ref[:, base : base + 384], 1, 0)
        raw = dot(first, w_ref[:, base + 384 : base + 512], 1, 0).astype(jnp.bfloat16).astype(jnp.float32)
        out_ref[half, :, 0:128] = turned(qkv[:, 0:128], cosine, sine).astype(jnp.bfloat16) * jnp.bfloat16(0.125)
        out_ref[half, :, 128:256] = turned(qkv[:, 128:256], cosine, sine).astype(jnp.bfloat16)
        blend = (0.5 * qkv[:, 256:384] + 0.5 * raw).astype(jnp.bfloat16)
        out_ref[half, :, 256:384] = blend
        blend = blend.astype(jnp.float32)
        power_ref[0:1, :] += jnp.sum(raw * raw, 0, keepdims=True)
        power_ref[1:2, :] += jnp.sum(blend * blend, 0, keepdims=True)


def project(h, first, weight, cosine, sine):
    n, width = h.shape
    rows = n // 2
    subs = rows // QB
    return pl.pallas_call(
        project_kernel,
        grid=(n // QB,),
        in_specs=[
            pl.BlockSpec((QB, width), lambda i: (i, 0)),
            pl.BlockSpec((QB, width), lambda i: (i, 0)),
            pl.BlockSpec(weight.shape, lambda i: (0, 0)),
            pl.BlockSpec((QB, 128), lambda i: (i, 0)),
            pl.BlockSpec((QB, 128), lambda i: (i, 0)),
        ],
        out_specs=[
            pl.BlockSpec((2, QB, 384), lambda i: (i // subs, i % subs, 0)),
            pl.BlockSpec((8, 128), lambda i: (0, 0)),
        ],
        out_shape=[
            jax.ShapeDtypeStruct((4, rows, 384), jnp.bfloat16),
            jax.ShapeDtypeStruct((8, 128), jnp.float32),
        ],
        compiler_params=pltpu.CompilerParams(vmem_limit_bytes=VMEM),
        cost_estimate=HINT,
    )(h, first, weight, cosine, sine)


def causal(scores, start, q_pos, i, rows, last):
    k_pos = i * rows + lax.broadcasted_iota(jnp.int32, scores.shape, 0)
    keep = k_pos >= start
    if last:
        keep = keep & (k_pos <= q_pos)
    return jnp.where(keep, scores, -1e30)


def attend_kernel(start_ref, q_ref, k_ref, v_ref, o_ref, lse_ref, *, pieces, rows):
    for j in range(pieces):
        for sub in range(rows // QB):
            first = j * rows + sub * QB
            q_pair = q_ref[j, sub * QB : (sub + 1) * QB, :]
            start = start_ref[0:1, first : first + QB]
            q_pos = first + lane_of((1, QB))
            outs = []
            for head in range(2):
                mine = lane_of(q_pair.shape) // HD == head
                qm = jnp.where(mine, q_pair, jnp.zeros_like(q_pair))
                blocks = []
                for i in range(j + 1):
                    n = rows if i < j else (sub + 1) * QB
                    s = dot(k_ref[i, :n, :], qm, 1, 1)
                    blocks.append((i, n, causal(s, start, q_pos, i, rows, i == j)))
                peak = functools.reduce(jnp.maximum, [jnp.max(b[2], 0, keepdims=True) for b in blocks])
                total = 0.0
                acc = 0.0
                for i, n, s in blocks:
                    p = jnp.exp(s - peak)
                    total = total + jnp.sum(p, 0, keepdims=True)
                    acc = acc + dot(v_ref[i, :n, :], p.astype(jnp.bfloat16), 0, 0)
                outs.append((acc / total)[head * HD : (head + 1) * HD])
                lse_ref[head : head + 1, first : first + QB] = peak + jnp.log(total)
            o_ref[j, sub * QB : (sub + 1) * QB, :] = jnp.transpose(jnp.concatenate(outs, 0)).astype(o_ref.dtype)


def column(pieces, rows, at):
    return pl.BlockSpec((pieces, rows, 128), lambda _: (0, 0, at))


def whole(shape):
    return pl.BlockSpec(shape, lambda _: (0,) * len(shape))


def attend(start, qkv):
    pieces, rows, _ = qkv.shape
    n = pieces * rows
    return pl.pallas_call(
        functools.partial(attend_kernel, pieces=pieces, rows=rows),
        grid=(1,),
        in_specs=[whole((1, n))] + [column(pieces, rows, i) for i in range(3)],
        out_specs=[whole((pieces, rows, 128)), whole((2, n))],
        out_shape=[
            jax.ShapeDtypeStruct((pieces, rows, 128), jnp.bfloat16),
            jax.ShapeDtypeStruct((2, n), jnp.float32),
        ],
        compiler_params=pltpu.CompilerParams(vmem_limit_bytes=VMEM),
        cost_estimate=HINT,
    )(start, qkv, qkv, qkv)


def back_kernel(
    start_ref, q_ref, k_ref, v_ref, o_ref, g_ref, lse_ref, flat_ref, cos_ref, sin_ref, d_ref, acc_k, acc_v, *, pieces, rows
):
    acc_k[...] = jnp.zeros_like(acc_k)
    acc_v[...] = jnp.zeros_like(acc_v)
    low = HD // 2
    for j in range(pieces):
        for sub in range(rows // QB):
            first = j * rows + sub * QB
            here = slice(sub * QB, (sub + 1) * QB)
            q_pair = q_ref[j, here, :]
            g_pair = g_ref[j, here, :]
            start = start_ref[0:1, first : first + QB]
            q_pos = first + lane_of((1, QB))
            inner = jnp.transpose(o_ref[j, here, :].astype(jnp.float32) * g_pair.astype(jnp.float32))
            cosine = flat_ref[0, :, first : first + QB]
            sine = flat_ref[1, :, first : first + QB]
            outs = []
            for head in range(2):
                mine = lane_of(q_pair.shape) // HD == head
                qm = jnp.where(mine, q_pair, jnp.zeros_like(q_pair))
                gm = jnp.where(mine, g_pair, jnp.zeros_like(g_pair))
                delta = jnp.sum(inner[head * HD : (head + 1) * HD], 0, keepdims=True)
                lse = lse_ref[head : head + 1, first : first + QB]
                acc = 0.0
                for i in range(j + 1):
                    n = rows if i < j else (sub + 1) * QB
                    k_blk = k_ref[i, :n, :]
                    s = causal(dot(k_blk, qm, 1, 1), start, q_pos, i, rows, i == j)
                    p = jnp.exp(s - lse)
                    dp = dot(v_ref[i, :n, :], gm, 1, 1)
                    ds = (p * (dp - delta)).astype(jnp.bfloat16)
                    acc_v[i, :n, :] += dot(p.astype(jnp.bfloat16), gm, 1, 0)
                    acc_k[i, :n, :] += dot(ds, qm, 1, 0)
                    acc = acc + dot(k_blk, ds, 0, 0)
                near = acc[head * HD : head * HD + low] * 0.125
                far = acc[head * HD + low : (head + 1) * HD] * 0.125
                outs += [near * cosine + far * sine, far * cosine - near * sine]
            d_ref[j, here, 0:128] = jnp.transpose(jnp.concatenate(outs, 0)).astype(d_ref.dtype)
    for j in range(pieces):
        here = slice(j * rows, (j + 1) * rows)
        d_ref[j, :, 128:256] = turned(acc_k[j], cos_ref[here, :], -sin_ref[here, :]).astype(d_ref.dtype)
        d_ref[j, :, 256:384] = acc_v[j].astype(d_ref.dtype) * jnp.bfloat16(0.5)


def attend_back(start, qkv, o, g, lse, flat, cosine, sine):
    pieces, rows, _ = qkv.shape
    n = pieces * rows
    one = whole((pieces, rows, 128))
    return pl.pallas_call(
        functools.partial(back_kernel, pieces=pieces, rows=rows),
        grid=(1,),
        in_specs=[whole((1, n))]
        + [column(pieces, rows, i) for i in range(3)]
        + [one, one, whole((2, n)), whole(flat.shape), whole((n, 128)), whole((n, 128))],
        out_specs=whole((pieces, rows, 384)),
        scratch_shapes=[pltpu.VMEM((pieces, rows, 128), jnp.float32)] * 2,
        out_shape=jax.ShapeDtypeStruct((pieces, rows, 384), jnp.bfloat16),
        compiler_params=pltpu.CompilerParams(vmem_limit_bytes=VMEM),
        cost_estimate=HINT,
    )(start, qkv, qkv, qkv, o, g, lse, flat, cosine, sine)


def rows_spec(block, width):
    return pl.BlockSpec((block, width), lambda i, *_: (i, 0))


def fixed(shape):
    return pl.BlockSpec(shape, lambda i, *_: (0,) * len(shape))


def mix_kernel(*refs, pairs, block):
    parts, (live_ref, w_ref, mixed_ref, out_ref) = refs[:pairs], refs[pairs:]
    live = live_ref[...]
    for q in range(2):
        for p in range(pairs):
            at = (q * pairs + p) * 128
            mixed_ref[:, at : at + 128] = parts[p][q] * live
    out_ref[...] = dot(mixed_ref[...], w_ref[...], 1, 0).astype(out_ref.dtype)


def mix(parts, live, weight):
    pairs = len(parts)
    rows = parts[0].shape[1]
    inner, width = weight.shape
    block = rows
    return pl.pallas_call(
        functools.partial(mix_kernel, pairs=pairs, block=block),
        grid=(2,),
        in_specs=[pl.BlockSpec((2, block, 128), lambda i: (i, 0, 0))] * pairs
        + [rows_spec(block, 1), fixed(weight.shape)],
        out_specs=[rows_spec(block, inner), rows_spec(block, width)],
        out_shape=[
            jax.ShapeDtypeStruct((2 * rows, inner), jnp.bfloat16),
            jax.ShapeDtypeStruct((2 * rows, width), jnp.bfloat16),
        ],
        compiler_params=pltpu.CompilerParams(vmem_limit_bytes=VMEM),
        cost_estimate=HINT,
    )(*parts, live, weight)


def feed_kernel(x_ref, mine_ref, other_ref, gain_ref, dy_ref, *refs):
    weights, (down_ref, res_ref, h_ref, hid_ref, d_ref, out_ref) = refs[:2], refs[2:]
    f32 = jnp.float32
    pad = down_ref.shape[0] // 2
    res = x_ref[...].astype(f32) + (mine_ref[...].astype(f32) + other_ref[...].astype(f32))
    res_ref[...] = res
    inverse = lax.rsqrt(jnp.mean(res * res, axis=-1, keepdims=True) + norm_eps)
    h = (res * inverse * gain_ref[...]).astype(jnp.bfloat16)
    h_ref[...] = h
    dy = dy_ref[...]
    for q in range(2):
        for at in range(0, pad, 256):
            near = slice(q * 2 * pad + at, q * 2 * pad + at + 256)
            far = slice(q * 2 * pad + pad + at, q * 2 * pad + pad + at + 256)
            here = slice(q * pad + at, q * pad + at + 256)
            gate = dot(h, weights[q][:, at : at + 256], 1, 0)
            up = dot(h, weights[q][:, pad + at : pad + at + 256], 1, 0)
            d_hid = dot(dy, down_ref[here, :], 1, 1).astype(jnp.bfloat16).astype(f32)
            sig = 1.0 / (1.0 + jnp.exp(-gate))
            silu = gate * sig
            hid_ref[:, here] = (silu * up).astype(jnp.bfloat16)
            d_ref[:, near] = (d_hid * up * (sig * (1.0 + gate * (1.0 - sig)))).astype(jnp.bfloat16)
            d_ref[:, far] = (d_hid * silu).astype(jnp.bfloat16)
    total = dot(d_ref[:, : 2 * pad], weights[0][:, : 2 * pad], 1, 1)
    total = total + dot(d_ref[:, 2 * pad :], weights[1][:, : 2 * pad], 1, 1)
    out_ref[...] = total.astype(jnp.bfloat16)


def feed(x, mine, other, gain, dy, weights, down):
    n, width = x.shape
    pad = down.shape[0] // 2
    span = weights.shape[1] // 2
    block = n // 4
    tokens = rows_spec(block, width)
    bf16 = jnp.bfloat16
    quarter = lambda q: pl.BlockSpec((width, span), lambda i: (0, q))
    return pl.pallas_call(
        feed_kernel,
        grid=(n // block,),
        in_specs=[tokens, tokens, tokens, fixed((1, width)), tokens, quarter(0), quarter(1), fixed(down.shape)],
        out_specs=[tokens, tokens, rows_spec(block, 2 * pad), rows_spec(block, 4 * pad), tokens],
        out_shape=[
            jax.ShapeDtypeStruct((n, width), jnp.float32),
            jax.ShapeDtypeStruct((n, width), bf16),
            jax.ShapeDtypeStruct((n, 2 * pad), bf16),
            jax.ShapeDtypeStruct((n, 4 * pad), bf16),
            jax.ShapeDtypeStruct((n, width), bf16),
        ],
        compiler_params=pltpu.CompilerParams(vmem_limit_bytes=VMEM),
        cost_estimate=HINT,
    )(x, mine, other, gain, dy, weights, weights, down)


def turn_kernel(core_ref, res_ref, mine_ref, other_ref, dy_ref, gain_ref, w_ref, live_ref, dres_ref, dattn_ref, gains_ref, *outs):
    f32 = jnp.float32
    pairs = len(outs)
    res = res_ref[...]
    inverse = lax.rsqrt(jnp.mean(res * res, axis=-1, keepdims=True) + norm_eps)
    normed = res * inverse
    grad = mine_ref[...].astype(f32) + other_ref[...].astype(f32)
    scaled = grad * gain_ref[...]
    d_res = dy_ref[...].astype(f32) + inverse * (scaled - normed * jnp.mean(scaled * normed, axis=-1, keepdims=True))
    dres_ref[...] = d_res
    d_attn = d_res.astype(jnp.bfloat16)
    dattn_ref[...] = d_attn
    mixed = dot(d_attn, w_ref[...], 1, 1).astype(jnp.bfloat16) * live_ref[...]
    for q in range(2):
        for p in range(pairs):
            at = (q * pairs + p) * 128
            outs[p][q] = mixed[:, at : at + 128]
    at = pl.program_id(0)

    @pl.when(at == 0)
    def _():
        gains_ref[...] = jnp.zeros_like(gains_ref)

    @pl.when(at // (pl.num_programs(0) // 2) == core_ref[0])
    def _():
        gains_ref[0:1, :] += jnp.sum(grad * normed, 0, keepdims=True)


def turn(core, res, mine, other, dy, gain, weight, live):
    n, width = res.shape
    inner = weight.shape[0]
    pairs = inner // 256
    rows = n // 2
    block = rows // 2
    subs = rows // block
    tokens = rows_spec(block, width)
    packed = pl.BlockSpec((2, block, 128), lambda i, *_: (i // subs, i % subs, 0))
    return pl.pallas_call(
        turn_kernel,
        grid_spec=pltpu.PrefetchScalarGridSpec(
            num_scalar_prefetch=1,
            grid=(n // block,),
            in_specs=[tokens] * 4 + [fixed((1, width)), fixed(weight.shape), rows_spec(block, 1)],
            out_specs=[tokens, tokens, fixed((8, width))] + [packed] * pairs,
        ),
        out_shape=[
            jax.ShapeDtypeStruct((n, width), jnp.float32),
            jax.ShapeDtypeStruct((n, width), jnp.bfloat16),
            jax.ShapeDtypeStruct((8, width), jnp.float32),
        ]
        + [jax.ShapeDtypeStruct((4, rows, 128), jnp.bfloat16)] * pairs,
        compiler_params=pltpu.CompilerParams(vmem_limit_bytes=VMEM),
        cost_estimate=HINT,
    )(core, res, mine, other, dy, gain, weight, live)


def weigh_kernel(a_ref, b_ref, out_ref):
    out_ref[...] = dot(a_ref[...], b_ref[...], 0, 0).astype(out_ref.dtype)


def weigh(a, b):
    n, left = a.shape
    right = b.shape[1]
    wide = next(w for w in (1024, 768, 512, 256, right) if right % w == 0)
    return pl.pallas_call(
        weigh_kernel,
        grid=(right // wide,),
        in_specs=[pl.BlockSpec((n, left), lambda i: (0, 0)), pl.BlockSpec((n, wide), lambda i: (0, i))],
        out_specs=pl.BlockSpec((left, wide), lambda i: (0, i)),
        out_shape=jax.ShapeDtypeStruct((left, right), jnp.bfloat16),
        compiler_params=pltpu.CompilerParams(vmem_limit_bytes=VMEM),
        cost_estimate=HINT,
    )(a, b)


def slices_kernel(slot_ref, *refs, pairs):
    ins, outs = refs[:4], refs[4:]
    for p in range(pairs):
        for i in range(4):
            outs[p][:, i * 128 : (i + 1) * 128] = ins[i][:, p * 128 : (p + 1) * 128]


def inner_slices(slot, weights, slots):
    width, cols = weights[0].shape
    rows, pairs = width // slots, cols // 128
    return pl.pallas_call(
        functools.partial(slices_kernel, pairs=pairs),
        grid_spec=pltpu.PrefetchScalarGridSpec(
            num_scalar_prefetch=1,
            grid=(1,),
            in_specs=[pl.BlockSpec((rows, cols), lambda i, slot: (slot[0], 0))] * 4,
            out_specs=[pl.BlockSpec((rows, 512), lambda i, slot: (0, 0))] * pairs,
        ),
        out_shape=[jax.ShapeDtypeStruct((rows, 512), jnp.bfloat16)] * pairs,
        compiler_params=pltpu.CompilerParams(vmem_limit_bytes=VMEM),
        cost_estimate=HINT,
    )(slot, *weights)


def spread_gu_kernel(sum_ref, gate_ref, up_ref):
    hid, pad = gate_ref.shape[0], sum_ref.shape[1] // 2
    gate_ref[...] = jnp.transpose(sum_ref[:, :hid].astype(jnp.float32))
    up_ref[...] = jnp.transpose(sum_ref[:, pad : pad + hid].astype(jnp.float32))


def spread_gu(total, pad, hid):
    n = total.shape[0]
    block = n // 4
    return pl.pallas_call(
        spread_gu_kernel,
        grid=(4,),
        in_specs=[rows_spec(block, 2 * pad)],
        out_specs=[pl.BlockSpec((hid, block), lambda i: (0, i))] * 2,
        out_shape=[jax.ShapeDtypeStruct((hid, n), jnp.float32)] * 2,
        compiler_params=pltpu.CompilerParams(vmem_limit_bytes=VMEM),
        cost_estimate=HINT,
    )(total)


def spread_do_kernel(sum_ref, down_ref, out_ref):
    n_down, n_out = down_ref.shape[0], out_ref.shape[0]
    down_ref[...] = sum_ref[:n_down, :].astype(jnp.float32)
    out_ref[...] = sum_ref[n_down : n_down + n_out, :].astype(jnp.float32)


def spread_do(total, slots, down_rows, out_rows, width):
    rows = total.shape[0] // slots
    shapes = [(down_rows, width), (out_rows, width)]
    return pl.pallas_call(
        spread_do_kernel,
        grid=(slots,),
        in_specs=[rows_spec(rows, width)],
        out_specs=[rows_spec(*s) for s in shapes],
        out_shape=[jax.ShapeDtypeStruct((s[0] * slots, s[1]), jnp.float32) for s in shapes],
        compiler_params=pltpu.CompilerParams(vmem_limit_bytes=VMEM),
        cost_estimate=HINT,
    )(total)


def inner_kernel(*refs):
    ins, outs = refs[:-4], refs[-4:]
    for p, ref in enumerate(ins):
        for i in range(4):
            outs[i][:, p * 128 : (p + 1) * 128] = ref[:, i * 128 : (i + 1) * 128].astype(jnp.float32)


def inner_spread(parts):
    n = parts[0][0].shape[0]
    block = n // 2
    cols = 128 * len(parts)
    at = lambda col: pl.BlockSpec((block, 512), lambda i: (i, col))
    return pl.pallas_call(
        inner_kernel,
        grid=(2,),
        in_specs=[at(col) for _, col in parts],
        out_specs=[rows_spec(block, cols)] * 4,
        out_shape=[jax.ShapeDtypeStruct((n, cols), jnp.float32)] * 4,
        compiler_params=pltpu.CompilerParams(vmem_limit_bytes=VMEM),
        cost_estimate=HINT,
    )(*(a for a, _ in parts))


def multiply_kernel(a_ref, b_ref, out_ref):
    out_ref[...] = dot(a_ref[...], b_ref[...], 1, 0).astype(out_ref.dtype)


def multiply(a, b):
    n, width = a.shape[0], b.shape[1]
    block = n // 4
    return pl.pallas_call(
        multiply_kernel,
        grid=(4,),
        in_specs=[rows_spec(block, a.shape[1]), fixed(b.shape)],
        out_specs=rows_spec(block, width),
        out_shape=jax.ShapeDtypeStruct((n, width), jnp.bfloat16),
        compiler_params=pltpu.CompilerParams(vmem_limit_bytes=VMEM),
        cost_estimate=HINT,
    )(a, b)


def moved(values, bit):
    return lax.ppermute(values, "dp", [(i, i ^ bit) for i in range(lax.axis_size("dp"))])


def cross_pairs(n_dp):
    pairs = []
    for d in range(n_dp):
        for z in range(4):
            pairs.append((d * 4 + z, d * 4 + (z ^ 1) if z // 2 == d % 2 else (d ^ 1) * 4 + (z ^ 2)))
    return pairs


def side_pairs(n_dp):
    return [(d * 4 + z, d * 4 + (z ^ 1)) for d in range(n_dp) for z in range(4) if z // 2 != d % 2]


def tied(values, *others):
    return lax.optimization_barrier((values, others))[0]


class Place:
    def __init__(self):
        self.n_dp = lax.axis_size("dp")
        self.slots = self.n_dp // 2
        self.d = lax.axis_index("dp")
        self.z = lax.axis_index("mp")
        self.core = self.d % 2
        self.slot = self.d // 2
        self.own = (self.z // 2) == self.core
        self.even = (self.z % 2) == 0
        self.sides = [[2 * i + c for i in range(self.slots)] for c in range(2)]

    def cross(self, values):
        return lax.ppermute(values, ("dp", "mp"), cross_pairs(self.n_dp))

    def side(self, values):
        return lax.ppermute(values, ("dp", "mp"), side_pairs(self.n_dp))

    def ordered(self, mine, other):
        return jnp.where(self.core == 0, jnp.concatenate([mine, other], 0), jnp.concatenate([other, mine], 0))

    def slice_of(self, weight):
        rows = weight.shape[0] // self.slots
        return lax.dynamic_slice_in_dim(weight, self.slot * rows, rows, 0)

    def quarters(self, part, got):
        far = self.side(got)
        first = jnp.where(self.own, part, got)
        second = jnp.where(self.own, got, far)
        return jnp.where(self.even, first, second), jnp.where(self.even, second, first)

    def gathered(self, part):
        return lax.all_gather(part, "dp", axis=0, tiled=True, axis_index_groups=self.sides)

    def gathered_direct(self, part):
        every = jnp.concatenate([part] * self.slots, 0)
        return lax.all_to_all(every, "dp", 0, 0, tiled=True, axis_index_groups=self.sides)

    def gathered_steps(self, part):
        if self.slots != 4:
            return self.gathered(part)
        rows = part.shape[0]
        every = jnp.zeros((4 * rows, part.shape[1]), part.dtype)
        for k, piece in enumerate((part, moved(part, 2), moved(part, 4), moved(part, 6))):
            every = lax.dynamic_update_slice_in_dim(every, piece, (self.slot ^ k) * rows, 0)
        return every

    def gathered_pairs(self, part):
        return lax.all_to_all(jnp.concatenate([part] * self.n_dp, 0), "dp", 0, 0, tiled=True)

    def scattered(self, values):
        return lax.psum_scatter(values, "dp", scatter_dimension=0, tiled=True, axis_index_groups=self.sides)

    def pieces(self, values):
        if self.slots != 4:
            return [self.scattered(values)]
        rows = values.shape[0] // 4
        pick = lambda k: lax.dynamic_slice_in_dim(values, (self.slot ^ k) * rows, rows, 0)
        return [pick(0), moved(pick(1), 2), moved(pick(2), 4), moved(pick(3), 6)]

    def added(self, parts):
        return sum(p.astype(jnp.float32) for p in parts).astype(jnp.bfloat16)

    def swapped(self, values):
        every = lax.all_to_all(values, "dp", 0, 0, tiled=True, axis_index_groups=self.sides)
        return list(every.reshape((self.slots, -1) + every.shape[1:]))

    def bring(self, low, high):
        first = jnp.where(self.even, low, high)
        second = jnp.where(self.even, high, low)
        return first, second, self.side(second)

    def bring_across(self, first, second, far):
        total = (first.astype(jnp.float32) + far.astype(jnp.float32)).astype(jnp.bfloat16)
        return self.cross(jnp.where(self.own, second, total))

    def bring_home(self, first, got):
        f32, bf16 = jnp.float32, jnp.bfloat16
        part = jnp.where(self.own, (first.astype(f32) + got.astype(f32)).astype(bf16), got)
        half = first.shape[0] // 2
        cut = lambda which: lax.dynamic_slice_in_dim(part, which * half, half, 0)
        return (cut(self.core).astype(f32) + moved(cut(1 - self.core), 1).astype(f32)).astype(bf16)


def exchanged(values):
    return lax.all_to_all(values, "mp", 0, 0, tiled=True)


def rms_parts(values):
    inverse = lax.rsqrt(jnp.mean(values * values, axis=-1, keepdims=True) + norm_eps)
    return (values * inverse, inverse)


def rms_back(grad_rows, normed, inverse, gain_vec):
    grad_normed = grad_rows * gain_vec
    return inverse * (grad_normed - normed * jnp.mean(grad_normed * normed, axis=-1, keepdims=True))


def mm(a, b):
    return dot(a, b, 1, 0)


def mm_t(a, b):
    return dot(a, b, 1, 1)


def t_mm(a, b):
    return dot(a, b, 0, 0)


def shards(
    hidden_in,
    first_in,
    segment_ids,
    valid_tokens,
    w_query,
    w_key,
    w_value,
    w_first_value,
    w_out,
    w_gate,
    w_up,
    w_down,
    gain_attn,
    gain_mlp,
    out_cotangent,
):
    at = Place()
    bf16, f32 = jnp.bfloat16, jnp.float32
    rows, width = hidden_in.shape
    cols = w_query.shape[1]
    pairs = cols // 128
    hid = w_gate.shape[1]
    pad = -(-hid // 256) * 256
    beside = lambda *parts: jnp.concatenate(parts, 1)

    slot = at.slot.reshape(1).astype(jnp.int32)
    parts = inner_slices(slot, (w_query, w_key, w_value, w_first_value), at.slots)
    down_rows, out_rows = hid // at.slots, cols // at.slots
    tall = width // at.slots
    got_pair = []
    before = ()
    for part in parts:
        part = tied(part, before)
        before = at.cross(part)
        got_pair.append((part, before))
    wider = jnp.zeros((tall, pad - hid), bf16)
    outer = jnp.concatenate(
        [at.slice_of(w_down), at.slice_of(w_out), jnp.zeros((tall - down_rows - out_rows, width), bf16)], 0
    )
    part = tied(beside(at.slice_of(w_gate), wider, at.slice_of(w_up), wider, outer), before)
    got_feed = (part, at.cross(part))
    near = [beside(*at.quarters(part, got)) for part, got in got_pair]
    w_pair = [at.gathered_direct(near[0])]

    x_all = at.ordered(*tied((hidden_in, moved(hidden_in, 1)), near[0]))
    first_all = at.ordered(*tied((first_in, moved(first_in, 1)), near[0]))
    facts = jnp.stack([segment_ids, valid_tokens])
    facts = tied(at.ordered(facts[None], moved(facts, 1)[None]), near[0])
    seq_places = jax.vmap(token_places)(facts[:, 0])
    live = lax.dynamic_slice_in_dim(facts[:, 1], at.z * rows, rows, 1).reshape(-1, 1).astype(bf16)
    places = lax.dynamic_slice_in_dim(seq_places, at.z * rows, rows, 1).reshape(-1)
    spots = jnp.arange(segment_ids.shape[0], dtype=jnp.int32)
    unit = at.z // 2
    unit_places = lax.dynamic_index_in_dim(seq_places, unit, 0, keepdims=False)
    unit_live = lax.dynamic_index_in_dim(facts[:, 1], unit, 0, keepdims=False)
    first_key = jnp.where(unit_live == 1, spots - unit_places, spots)[None]
    frequency = jnp.exp(jnp.arange(HD // 2, dtype=f32) * (-2.0 * math.log(10000.0) / HD))
    angles = jnp.concatenate([places, unit_places]).astype(f32)[None, :] * frequency[:, None]
    cos_flat, sin_flat = jnp.cos(angles), jnp.sin(angles)
    n_here = 2 * rows
    cosine = jnp.concatenate([cos_flat] * 4, 0).T
    sine = jnp.concatenate([-sin_flat, sin_flat] * 2, 0).T
    flat = jnp.stack([cos_flat[:, n_here:], sin_flat[:, n_here:]])

    normed_one, inverse_one = rms_parts(x_all.astype(f32))
    h_one = (normed_one * gain_attn).astype(bf16)
    kept = []
    mixed = []
    powers = 0.0
    sends = []
    for p in range(pairs):
        if p == 1:
            part, got = got_feed
            feed_part = tied(beside(*at.quarters(part, got)), (sends, first_key, flat, cosine, sine))
        if p:
            w_pair.append(at.gathered_steps(tied(near[p], feed_part)))
        sent, power = project(h_one, first_all, w_pair[p], cosine[:n_here], sine[:n_here])
        powers = powers + jnp.sum(power, 1)
        sends.append(sent)
    full = at.gathered(feed_part)
    span = 2 * pad + width
    both_do = full.reshape(at.slots, tall, 2 * span)
    lanes = lambda q: slice(q * span + 2 * pad, (q + 1) * span)
    nothing = jnp.zeros((pad - hid, width), bf16)
    full_d = jnp.concatenate(
        [a for q in range(2) for a in (both_do[:, :down_rows, lanes(q)].reshape(hid, width), nothing)], 0
    )
    full_o = jnp.concatenate(
        [both_do[:, down_rows : down_rows + out_rows, lanes(q)].reshape(cols, width) for q in range(2)], 0
    )

    for p in range(pairs):
        qkv = exchanged(sends[p])
        attended, logsum = attend(first_key, qkv)
        kept.append((qkv, attended, logsum))
        mixed.append(exchanged(attended))
    dy_own = tied(lax.dynamic_slice_in_dim(out_cotangent, at.z * rows, rows, 0), sends)
    dy_all = at.ordered(dy_own, moved(dy_own, 1))

    own_rows = lambda a: lax.dynamic_slice_in_dim(a, at.core * rows, rows, 0)
    other_rows = lambda a: lax.dynamic_slice_in_dim(a, (1 - at.core) * rows, rows, 0)

    attn_mixed, out_part = mix(mixed, live, full_o)
    residual, h_two, hidden, d_gu, d_part = feed(
        x_all, out_part, moved(out_part, 1), gain_mlp[None], dy_all, full, full_d
    )
    d_other = moved(d_part, 1)
    g_gu = weigh(h_two, d_gu)
    s_gu = at.scattered(g_gu)
    d_res, d_attn, gains, *sends = turn(
        at.core.reshape(1), tied(residual, g_gu), d_part, d_other, dy_all, gain_mlp[None], full_o, live
    )
    incoming = [exchanged(sent) for sent in sends]

    g_down = weigh(tied(hidden, sends), dy_all)
    g_out = weigh(attn_mixed, d_attn)
    blank = jnp.zeros((at.slots, tall - down_rows - out_rows, width), bf16)
    slotted = lambda g, first, n: g[first : first + n].reshape(at.slots, n // at.slots, width)
    g_do = jnp.concatenate(
        [
            jnp.concatenate([slotted(g_down, q * pad, hid), slotted(g_out, q * cols, cols), blank], 1)
            for q in range(2)
        ],
        2,
    ).reshape(-1, 2 * width)
    s_do = at.scattered(g_do)
    backs = []
    key = tied(first_key, (g_down, g_out))
    for p in range(pairs):
        qkv, attended, logsum = kept[p]
        back = attend_back(key, qkv, attended, incoming[p], logsum, flat, cosine[n_here:], sine[n_here:])
        backs.append(exchanged(back))
        if p == 0:
            ffn = multiply(tied(hidden, back), full_d)
            tied_gu = tied(s_gu, back)
            first_gu, second_gu, far_gu = at.bring(tied_gu[:, : 2 * pad], tied_gu[:, 2 * pad :])
            key = tied(key, (far_gu, ffn))
    got_gu = at.bring_across(first_gu, second_gu, far_gu)
    near_gu = at.bring_home(first_gu, got_gu)
    ffn = own_rows(ffn).astype(f32) + moved(other_rows(ffn), 1).astype(f32)
    block_out = (own_rows(residual) + ffn).astype(bf16)

    d_h1 = 0.0
    parts = []
    sent_pair = ()
    for p in range(pairs):
        back = tied(backs[p], (block_out, got_gu, sent_pair))
        d_inner = jnp.concatenate([beside(back[2 * s], back[2 * s + 1]) for s in range(2)], 0)
        d_first = beside(d_inner[:, 256:384], d_inner[:, 640:768])
        w_inner = beside(w_pair[p][:, :384], w_pair[p][:, 512:896])
        d_h1 = d_h1 + mm_t(d_inner, w_inner)
        g_inner = weigh(h_one, d_inner)
        g_first = weigh(first_all, d_first)
        g_pair = beside(g_inner[:, :384], g_first[:, :128], g_inner[:, 384:], g_first[:, 128:])
        parts.append(at.swapped(g_pair) if p else at.pieces(g_pair))
        sent_pair = g_pair
    d_h1 = d_h1.astype(bf16)
    d_h1 = own_rows(d_h1).astype(f32) + moved(other_rows(d_h1), 1).astype(f32)
    own_normed = own_rows(normed_one)
    grad_input = (own_rows(d_res) + rms_back(d_h1, own_normed, own_rows(inverse_one), gain_attn)).astype(bf16)

    gain_parts = jnp.stack([jnp.sum(d_h1 * own_normed, 0), gains[0]])
    small = jnp.concatenate([gain_parts.reshape(-1), powers[:2], jnp.zeros((126,), f32)])
    small = small.reshape(-1, 128)
    small = jnp.pad(small, ((0, -small.shape[0] % 8), (0, 0)))
    for axis, size in (("dp", at.n_dp), ("mp", 4)):
        every = lax.all_to_all(jnp.concatenate([small] * size, 0), axis, 0, 0, tiled=True)
        small = jnp.sum(every.reshape((size,) + small.shape), 0)
    sum_gu = lax.all_gather(near_gu, "dp", axis=0, tiled=True)
    most = at.added(tied(parts[0], backs))
    first, second, far = at.bring(
        *(beside(tied(s_do, back)[:, q * width : (q + 1) * width], most[:, q * 512 : (q + 1) * 512]) for q in range(2))
    )
    got = at.bring_across(first, second, tied(far, (parts, d_h1)))
    late = [at.added(part) for part in parts[1:]]
    late = [at.bring(part[:, :512], part[:, 512:]) for part in late]
    most = at.bring_home(first, tied(got, (late, sum_gu)))
    sum_do = lax.all_gather(most, "dp", axis=0, tiled=True)
    late = [at.bring_home(one, at.bring_across(one, two, tied(three, small))) for one, two, three in late]
    grad_gate, grad_up = spread_gu(sum_gu, pad, hid)
    inner_sums = [(sum_do, width // 512)]
    inner_sums += [(at.gathered_pairs(tied(part, (grad_gate, grad_up))), 0) for part in late]
    if down_rows % 16 == 0:
        grad_down, grad_out = spread_do(sum_do, at.slots, down_rows, out_rows, width)
    else:
        all_do = sum_do[:, :width].reshape(at.slots, tall, width)
        grad_down = all_do[:, :down_rows].reshape(hid, width).astype(f32)
        grad_out = all_do[:, down_rows : down_rows + out_rows].reshape(cols, width).astype(f32)
    small = small.reshape(-1)
    count = float(rows * at.n_dp * 4 * width)
    return (
        block_out,
        grad_input,
        *inner_spread(inner_sums),
        grad_out,
        grad_gate.T,
        grad_up.T,
        grad_down,
        small[:width],
        small[width : 2 * width],
        small[2 * width] / count,
        small[2 * width + 1] / count,
    )


def solution(mesh):
    placed = (
        P(("dp", "mp"), None),
        P(("dp", "mp"), None),
        P("dp"),
        P("dp"),
        P(None, "mp"),
        P(None, "mp"),
        P(None, "mp"),
        P(None, "mp"),
        P("mp", None),
        P(None, "mp"),
        P(None, "mp"),
        P("mp", None),
        P(),
        P(),
        P("dp", None),
    )
    return jax.shard_map(
        shards,
        mesh=mesh,
        in_specs=placed,
        out_specs=(
            P(("dp", "mp"), None),
            P(("dp", "mp"), None),
            P(None, "mp"),
            P(None, "mp"),
            P(None, "mp"),
            P(None, "mp"),
            P("mp", None),
            P(None, "mp"),
            P(None, "mp"),
            P("mp", None),
            P(),
            P(),
            P(),
            P(),
        ),
        check_vma=False,
    )
```

```python
import functools
import math

import jax
import jax.numpy as jnp
from jax import lax
from jax.experimental import pallas as pl
from jax.experimental.pallas import tpu as pltpu
from jax.sharding import PartitionSpec as P

HD = 64
norm_eps = 1e-06


def token_places(segment_ids):
    n_tokens = segment_ids.shape[0]
    indices = jnp.arange(n_tokens, dtype=jnp.int32)
    starts_new = jnp.concatenate([jnp.ones((1,), jnp.bool_), segment_ids[1:] != segment_ids[:-1]])
    begins = lax.cummax(jnp.where(starts_new, indices, jnp.zeros_like(indices)), axis=0)
    return indices - begins


QB = 256
VMEM = 48 * 2**20
HINT = pl.CostEstimate(flops=0, bytes_accessed=0, transcendentals=0)


def dot(a, b, ca, cb):
    return lax.dot_general(a, b, (((ca,), (cb,)), ((), ())), preferred_element_type=jnp.float32)


def lane_of(shape):
    return lax.broadcasted_iota(jnp.int32, shape, 1)


def turned(values, cosine, sine):
    near = lane_of(values.shape) % HD < HD // 2
    swapped = jnp.where(near, pltpu.roll(values, 128 - HD // 2, 1), pltpu.roll(values, HD // 2, 1))
    return values * cosine + swapped * sine


def project_kernel(h_ref, first_ref, w_ref, cos_ref, sin_ref, out_ref, power_ref):
    h, first = h_ref[...], first_ref[...]
    cosine, sine = cos_ref[...], sin_ref[...]
    at = pl.program_id(0)

    @pl.when(at == 0)
    def _():
        power_ref[...] = jnp.zeros_like(power_ref)

    for half in range(2):
        base = half * 512
        qkv = dot(h, w_ref[:, base : base + 384], 1, 0)
        raw = dot(first, w_ref[:, base + 384 : base + 512], 1, 0).astype(jnp.bfloat16).astype(jnp.float32)
        out_ref[half, :, 0:128] = turned(qkv[:, 0:128], cosine, sine).astype(jnp.bfloat16) * jnp.bfloat16(0.125)
        out_ref[half, :, 128:256] = turned(qkv[:, 128:256], cosine, sine).astype(jnp.bfloat16)
        blend = (0.5 * qkv[:, 256:384] + 0.5 * raw).astype(jnp.bfloat16)
        out_ref[half, :, 256:384] = blend
        blend = blend.astype(jnp.float32)
        power_ref[0:1, :] += jnp.sum(raw * raw, 0, keepdims=True)
        power_ref[1:2, :] += jnp.sum(blend * blend, 0, keepdims=True)


def project(h, first, weight, cosine, sine):
    n, width = h.shape
    rows = n // 2
    subs = rows // QB
    return pl.pallas_call(
        project_kernel,
        grid=(n // QB,),
        in_specs=[
            pl.BlockSpec((QB, width), lambda i: (i, 0)),
            pl.BlockSpec((QB, width), lambda i: (i, 0)),
            pl.BlockSpec(weight.shape, lambda i: (0, 0)),
            pl.BlockSpec((QB, 128), lambda i: (i, 0)),
            pl.BlockSpec((QB, 128), lambda i: (i, 0)),
        ],
        out_specs=[
            pl.BlockSpec((2, QB, 384), lambda i: (i // subs, i % subs, 0)),
            pl.BlockSpec((8, 128), lambda i: (0, 0)),
        ],
        out_shape=[
            jax.ShapeDtypeStruct((4, rows, 384), jnp.bfloat16),
            jax.ShapeDtypeStruct((8, 128), jnp.float32),
        ],
        compiler_params=pltpu.CompilerParams(vmem_limit_bytes=VMEM),
        cost_estimate=HINT,
    )(h, first, weight, cosine, sine)


def causal(scores, start, q_pos, i, rows, last):
    k_pos = i * rows + lax.broadcasted_iota(jnp.int32, scores.shape, 0)
    keep = k_pos >= start
    if last:
        keep = keep & (k_pos <= q_pos)
    return jnp.where(keep, scores, -1e30)


def attend_kernel(start_ref, q_ref, k_ref, v_ref, o_ref, lse_ref, *, pieces, rows):
    for j in range(pieces):
        for sub in range(rows // QB):
            first = j * rows + sub * QB
            q_pair = q_ref[j, sub * QB : (sub + 1) * QB, :]
            start = start_ref[0:1, first : first + QB]
            q_pos = first + lane_of((1, QB))
            outs = []
            for head in range(2):
                mine = lane_of(q_pair.shape) // HD == head
                qm = jnp.where(mine, q_pair, jnp.zeros_like(q_pair))
                blocks = []
                for i in range(j + 1):
                    n = rows if i < j else (sub + 1) * QB
                    s = dot(k_ref[i, :n, :], qm, 1, 1)
                    blocks.append((i, n, causal(s, start, q_pos, i, rows, i == j)))
                peak = functools.reduce(jnp.maximum, [jnp.max(b[2], 0, keepdims=True) for b in blocks])
                total = 0.0
                acc = 0.0
                for i, n, s in blocks:
                    p = jnp.exp(s - peak)
                    total = total + jnp.sum(p, 0, keepdims=True)
                    acc = acc + dot(v_ref[i, :n, :], p.astype(jnp.bfloat16), 0, 0)
                outs.append((acc / total)[head * HD : (head + 1) * HD])
                lse_ref[head : head + 1, first : first + QB] = peak + jnp.log(total)
            o_ref[j, sub * QB : (sub + 1) * QB, :] = jnp.transpose(jnp.concatenate(outs, 0)).astype(o_ref.dtype)


def column(pieces, rows, at):
    return pl.BlockSpec((pieces, rows, 128), lambda _: (0, 0, at))


def whole(shape):
    return pl.BlockSpec(shape, lambda _: (0,) * len(shape))


def attend(start, qkv):
    pieces, rows, _ = qkv.shape
    n = pieces * rows
    return pl.pallas_call(
        functools.partial(attend_kernel, pieces=pieces, rows=rows),
        grid=(1,),
        in_specs=[whole((1, n))] + [column(pieces, rows, i) for i in range(3)],
        out_specs=[whole((pieces, rows, 128)), whole((2, n))],
        out_shape=[
            jax.ShapeDtypeStruct((pieces, rows, 128), jnp.bfloat16),
            jax.ShapeDtypeStruct((2, n), jnp.float32),
        ],
        compiler_params=pltpu.CompilerParams(vmem_limit_bytes=VMEM),
        cost_estimate=HINT,
    )(start, qkv, qkv, qkv)


def back_kernel(
    start_ref, q_ref, k_ref, v_ref, o_ref, g_ref, lse_ref, flat_ref, cos_ref, sin_ref, d_ref, acc_k, acc_v, *, pieces, rows
):
    acc_k[...] = jnp.zeros_like(acc_k)
    acc_v[...] = jnp.zeros_like(acc_v)
    low = HD // 2
    for j in range(pieces):
        for sub in range(rows // QB):
            first = j * rows + sub * QB
            here = slice(sub * QB, (sub + 1) * QB)
            q_pair = q_ref[j, here, :]
            g_pair = g_ref[j, here, :]
            start = start_ref[0:1, first : first + QB]
            q_pos = first + lane_of((1, QB))
            inner = jnp.transpose(o_ref[j, here, :].astype(jnp.float32) * g_pair.astype(jnp.float32))
            cosine = flat_ref[0, :, first : first + QB]
            sine = flat_ref[1, :, first : first + QB]
            outs = []
            for head in range(2):
                mine = lane_of(q_pair.shape) // HD == head
                qm = jnp.where(mine, q_pair, jnp.zeros_like(q_pair))
                gm = jnp.where(mine, g_pair, jnp.zeros_like(g_pair))
                delta = jnp.sum(inner[head * HD : (head + 1) * HD], 0, keepdims=True)
                lse = lse_ref[head : head + 1, first : first + QB]
                acc = 0.0
                for i in range(j + 1):
                    n = rows if i < j else (sub + 1) * QB
                    k_blk = k_ref[i, :n, :]
                    s = causal(dot(k_blk, qm, 1, 1), start, q_pos, i, rows, i == j)
                    p = jnp.exp(s - lse)
                    dp = dot(v_ref[i, :n, :], gm, 1, 1)
                    ds = (p * (dp - delta)).astype(jnp.bfloat16)
                    acc_v[i, :n, :] += dot(p.astype(jnp.bfloat16), gm, 1, 0)
                    acc_k[i, :n, :] += dot(ds, qm, 1, 0)
                    acc = acc + dot(k_blk, ds, 0, 0)
                near = acc[head * HD : head * HD + low] * 0.125
                far = acc[head * HD + low : (head + 1) * HD] * 0.125
                outs += [near * cosine + far * sine, far * cosine - near * sine]
            d_ref[j, here, 0:128] = jnp.transpose(jnp.concatenate(outs, 0)).astype(d_ref.dtype)
    for j in range(pieces):
        here = slice(j * rows, (j + 1) * rows)
        d_ref[j, :, 128:256] = turned(acc_k[j], cos_ref[here, :], -sin_ref[here, :]).astype(d_ref.dtype)
        d_ref[j, :, 256:384] = acc_v[j].astype(d_ref.dtype) * jnp.bfloat16(0.5)


def attend_back(start, qkv, o, g, lse, flat, cosine, sine):
    pieces, rows, _ = qkv.shape
    n = pieces * rows
    one = whole((pieces, rows, 128))
    return pl.pallas_call(
        functools.partial(back_kernel, pieces=pieces, rows=rows),
        grid=(1,),
        in_specs=[whole((1, n))]
        + [column(pieces, rows, i) for i in range(3)]
        + [one, one, whole((2, n)), whole(flat.shape), whole((n, 128)), whole((n, 128))],
        out_specs=whole((pieces, rows, 384)),
        scratch_shapes=[pltpu.VMEM((pieces, rows, 128), jnp.float32)] * 2,
        out_shape=jax.ShapeDtypeStruct((pieces, rows, 384), jnp.bfloat16),
        compiler_params=pltpu.CompilerParams(vmem_limit_bytes=VMEM),
        cost_estimate=HINT,
    )(start, qkv, qkv, qkv, o, g, lse, flat, cosine, sine)


def rows_spec(block, width):
    return pl.BlockSpec((block, width), lambda i, *_: (i, 0))


def fixed(shape):
    return pl.BlockSpec(shape, lambda i, *_: (0,) * len(shape))


def mix_kernel(*refs, pairs, block):
    parts, (live_ref, w_ref, mixed_ref, out_ref) = refs[:pairs], refs[pairs:]
    live = live_ref[...]
    for q in range(2):
        for p in range(pairs):
            at = (q * pairs + p) * 128
            mixed_ref[:, at : at + 128] = parts[p][q] * live
    out_ref[...] = dot(mixed_ref[...], w_ref[...], 1, 0).astype(out_ref.dtype)


def mix(parts, live, weight):
    pairs = len(parts)
    rows = parts[0].shape[1]
    inner, width = weight.shape
    block = rows
    return pl.pallas_call(
        functools.partial(mix_kernel, pairs=pairs, block=block),
        grid=(2,),
        in_specs=[pl.BlockSpec((2, block, 128), lambda i: (i, 0, 0))] * pairs
        + [rows_spec(block, 1), fixed(weight.shape)],
        out_specs=[rows_spec(block, inner), rows_spec(block, width)],
        out_shape=[
            jax.ShapeDtypeStruct((2 * rows, inner), jnp.bfloat16),
            jax.ShapeDtypeStruct((2 * rows, width), jnp.bfloat16),
        ],
        compiler_params=pltpu.CompilerParams(vmem_limit_bytes=VMEM),
        cost_estimate=HINT,
    )(*parts, live, weight)


def feed_kernel(x_ref, mine_ref, other_ref, gain_ref, dy_ref, *refs):
    weights, (down_ref, res_ref, h_ref, hid_ref, d_ref, out_ref) = refs[:2], refs[2:]
    f32 = jnp.float32
    pad = down_ref.shape[0] // 2
    res = x_ref[...].astype(f32) + (mine_ref[...].astype(f32) + other_ref[...].astype(f32))
    res_ref[...] = res
    inverse = lax.rsqrt(jnp.mean(res * res, axis=-1, keepdims=True) + norm_eps)
    h = (res * inverse * gain_ref[...]).astype(jnp.bfloat16)
    h_ref[...] = h
    dy = dy_ref[...]
    for q in range(2):
        for at in range(0, pad, 256):
            near = slice(q * 2 * pad + at, q * 2 * pad + at + 256)
            far = slice(q * 2 * pad + pad + at, q * 2 * pad + pad + at + 256)
            here = slice(q * pad + at, q * pad + at + 256)
            gate = dot(h, weights[q][:, at : at + 256], 1, 0)
            up = dot(h, weights[q][:, pad + at : pad + at + 256], 1, 0)
            d_hid = dot(dy, down_ref[here, :], 1, 1).astype(jnp.bfloat16).astype(f32)
            sig = 1.0 / (1.0 + jnp.exp(-gate))
            silu = gate * sig
            hid_ref[:, here] = (silu * up).astype(jnp.bfloat16)
            d_ref[:, near] = (d_hid * up * (sig * (1.0 + gate * (1.0 - sig)))).astype(jnp.bfloat16)
            d_ref[:, far] = (d_hid * silu).astype(jnp.bfloat16)
    total = dot(d_ref[:, : 2 * pad], weights[0][:, : 2 * pad], 1, 1)
    total = total + dot(d_ref[:, 2 * pad :], weights[1][:, : 2 * pad], 1, 1)
    out_ref[...] = total.astype(jnp.bfloat16)


def feed(x, mine, other, gain, dy, weights, down):
    n, width = x.shape
    pad = down.shape[0] // 2
    span = weights.shape[1] // 2
    block = n // 4
    tokens = rows_spec(block, width)
    bf16 = jnp.bfloat16
    quarter = lambda q: pl.BlockSpec((width, span), lambda i: (0, q))
    return pl.pallas_call(
        feed_kernel,
        grid=(n // block,),
        in_specs=[tokens, tokens, tokens, fixed((1, width)), tokens, quarter(0), quarter(1), fixed(down.shape)],
        out_specs=[tokens, tokens, rows_spec(block, 2 * pad), rows_spec(block, 4 * pad), tokens],
        out_shape=[
            jax.ShapeDtypeStruct((n, width), jnp.float32),
            jax.ShapeDtypeStruct((n, width), bf16),
            jax.ShapeDtypeStruct((n, 2 * pad), bf16),
            jax.ShapeDtypeStruct((n, 4 * pad), bf16),
            jax.ShapeDtypeStruct((n, width), bf16),
        ],
        compiler_params=pltpu.CompilerParams(vmem_limit_bytes=VMEM),
        cost_estimate=HINT,
    )(x, mine, other, gain, dy, weights, weights, down)


def turn_kernel(core_ref, res_ref, mine_ref, other_ref, dy_ref, gain_ref, w_ref, live_ref, dres_ref, dattn_ref, gains_ref, *outs):
    f32 = jnp.float32
    pairs = len(outs)
    res = res_ref[...]
    inverse = lax.rsqrt(jnp.mean(res * res, axis=-1, keepdims=True) + norm_eps)
    normed = res * inverse
    grad = mine_ref[...].astype(f32) + other_ref[...].astype(f32)
    scaled = grad * gain_ref[...]
    d_res = dy_ref[...].astype(f32) + inverse * (scaled - normed * jnp.mean(scaled * normed, axis=-1, keepdims=True))
    dres_ref[...] = d_res
    d_attn = d_res.astype(jnp.bfloat16)
    dattn_ref[...] = d_attn
    mixed = dot(d_attn, w_ref[...], 1, 1).astype(jnp.bfloat16) * live_ref[...]
    for q in range(2):
        for p in range(pairs):
            at = (q * pairs + p) * 128
            outs[p][q] = mixed[:, at : at + 128]
    at = pl.program_id(0)

    @pl.when(at == 0)
    def _():
        gains_ref[...] = jnp.zeros_like(gains_ref)

    @pl.when(at // (pl.num_programs(0) // 2) == core_ref[0])
    def _():
        gains_ref[0:1, :] += jnp.sum(grad * normed, 0, keepdims=True)


def turn(core, res, mine, other, dy, gain, weight, live):
    n, width = res.shape
    inner = weight.shape[0]
    pairs = inner // 256
    rows = n // 2
    block = rows // 2
    subs = rows // block
    tokens = rows_spec(block, width)
    packed = pl.BlockSpec((2, block, 128), lambda i, *_: (i // subs, i % subs, 0))
    return pl.pallas_call(
        turn_kernel,
        grid_spec=pltpu.PrefetchScalarGridSpec(
            num_scalar_prefetch=1,
            grid=(n // block,),
            in_specs=[tokens] * 4 + [fixed((1, width)), fixed(weight.shape), rows_spec(block, 1)],
            out_specs=[tokens, tokens, fixed((8, width))] + [packed] * pairs,
        ),
        out_shape=[
            jax.ShapeDtypeStruct((n, width), jnp.float32),
            jax.ShapeDtypeStruct((n, width), jnp.bfloat16),
            jax.ShapeDtypeStruct((8, width), jnp.float32),
        ]
        + [jax.ShapeDtypeStruct((4, rows, 128), jnp.bfloat16)] * pairs,
        compiler_params=pltpu.CompilerParams(vmem_limit_bytes=VMEM),
        cost_estimate=HINT,
    )(core, res, mine, other, dy, gain, weight, live)


def weigh_kernel(a_ref, b_ref, out_ref):
    out_ref[...] = dot(a_ref[...], b_ref[...], 0, 0).astype(out_ref.dtype)


def weigh(a, b):
    n, left = a.shape
    right = b.shape[1]
    wide = next(w for w in (1024, 768, 512, 256, right) if right % w == 0)
    return pl.pallas_call(
        weigh_kernel,
        grid=(right // wide,),
        in_specs=[pl.BlockSpec((n, left), lambda i: (0, 0)), pl.BlockSpec((n, wide), lambda i: (0, i))],
        out_specs=pl.BlockSpec((left, wide), lambda i: (0, i)),
        out_shape=jax.ShapeDtypeStruct((left, right), jnp.bfloat16),
        compiler_params=pltpu.CompilerParams(vmem_limit_bytes=VMEM),
        cost_estimate=HINT,
    )(a, b)


def slices_kernel(slot_ref, *refs, pairs):
    ins, outs = refs[:4], refs[4:]
    for p in range(pairs):
        for i in range(4):
            outs[p][:, i * 128 : (i + 1) * 128] = ins[i][:, p * 128 : (p + 1) * 128]


def inner_slices(slot, weights, slots):
    width, cols = weights[0].shape
    rows, pairs = width // slots, cols // 128
    return pl.pallas_call(
        functools.partial(slices_kernel, pairs=pairs),
        grid_spec=pltpu.PrefetchScalarGridSpec(
            num_scalar_prefetch=1,
            grid=(1,),
            in_specs=[pl.BlockSpec((rows, cols), lambda i, slot: (slot[0], 0))] * 4,
            out_specs=[pl.BlockSpec((rows, 512), lambda i, slot: (0, 0))] * pairs,
        ),
        out_shape=[jax.ShapeDtypeStruct((rows, 512), jnp.bfloat16)] * pairs,
        compiler_params=pltpu.CompilerParams(vmem_limit_bytes=VMEM),
        cost_estimate=HINT,
    )(slot, *weights)


def spread_gu_kernel(sum_ref, gate_ref, up_ref):
    hid, pad = gate_ref.shape[0], sum_ref.shape[1] // 2
    gate_ref[...] = jnp.transpose(sum_ref[:, :hid].astype(jnp.float32))
    up_ref[...] = jnp.transpose(sum_ref[:, pad : pad + hid].astype(jnp.float32))


def spread_gu(total, pad, hid):
    n = total.shape[0]
    block = n // 4
    return pl.pallas_call(
        spread_gu_kernel,
        grid=(4,),
        in_specs=[rows_spec(block, 2 * pad)],
        out_specs=[pl.BlockSpec((hid, block), lambda i: (0, i))] * 2,
        out_shape=[jax.ShapeDtypeStruct((hid, n), jnp.float32)] * 2,
        compiler_params=pltpu.CompilerParams(vmem_limit_bytes=VMEM),
        cost_estimate=HINT,
    )(total)


def spread_do_kernel(sum_ref, down_ref, out_ref):
    n_down, n_out = down_ref.shape[0], out_ref.shape[0]
    down_ref[...] = sum_ref[:n_down, :].astype(jnp.float32)
    out_ref[...] = sum_ref[n_down : n_down + n_out, :].astype(jnp.float32)


def spread_do(total, slots, down_rows, out_rows, width):
    rows = total.shape[0] // slots
    shapes = [(down_rows, width), (out_rows, width)]
    return pl.pallas_call(
        spread_do_kernel,
        grid=(slots,),
        in_specs=[rows_spec(rows, width)],
        out_specs=[rows_spec(*s) for s in shapes],
        out_shape=[jax.ShapeDtypeStruct((s[0] * slots, s[1]), jnp.float32) for s in shapes],
        compiler_params=pltpu.CompilerParams(vmem_limit_bytes=VMEM),
        cost_estimate=HINT,
    )(total)


def inner_kernel(*refs):
    ins, outs = refs[:-4], refs[-4:]
    for p, ref in enumerate(ins):
        for i in range(4):
            outs[i][:, p * 128 : (p + 1) * 128] = ref[:, i * 128 : (i + 1) * 128].astype(jnp.float32)


def inner_spread(parts):
    n = parts[0][0].shape[0]
    block = n // 2
    cols = 128 * len(parts)
    at = lambda col: pl.BlockSpec((block, 512), lambda i: (i, col))
    return pl.pallas_call(
        inner_kernel,
        grid=(2,),
        in_specs=[at(col) for _, col in parts],
        out_specs=[rows_spec(block, cols)] * 4,
        out_shape=[jax.ShapeDtypeStruct((n, cols), jnp.float32)] * 4,
        compiler_params=pltpu.CompilerParams(vmem_limit_bytes=VMEM),
        cost_estimate=HINT,
    )(*(a for a, _ in parts))


def multiply_kernel(a_ref, b_ref, out_ref):
    out_ref[...] = dot(a_ref[...], b_ref[...], 1, 0).astype(out_ref.dtype)


def multiply(a, b):
    n, width = a.shape[0], b.shape[1]
    block = n // 4
    return pl.pallas_call(
        multiply_kernel,
        grid=(4,),
        in_specs=[rows_spec(block, a.shape[1]), fixed(b.shape)],
        out_specs=rows_spec(block, width),
        out_shape=jax.ShapeDtypeStruct((n, width), jnp.bfloat16),
        compiler_params=pltpu.CompilerParams(vmem_limit_bytes=VMEM),
        cost_estimate=HINT,
    )(a, b)


def moved(values, bit):
    return lax.ppermute(values, "dp", [(i, i ^ bit) for i in range(lax.axis_size("dp"))])


def cross_pairs(n_dp):
    pairs = []
    for d in range(n_dp):
        for z in range(4):
            pairs.append((d * 4 + z, d * 4 + (z ^ 1) if z // 2 == d % 2 else (d ^ 1) * 4 + (z ^ 2)))
    return pairs


def side_pairs(n_dp):
    return [(d * 4 + z, d * 4 + (z ^ 1)) for d in range(n_dp) for z in range(4) if z // 2 != d % 2]


def tied(values, *others):
    return lax.optimization_barrier((values, others))[0]


class Place:
    def __init__(self):
        self.n_dp = lax.axis_size("dp")
        self.slots = self.n_dp // 2
        self.d = lax.axis_index("dp")
        self.z = lax.axis_index("mp")
        self.core = self.d % 2
        self.slot = self.d // 2
        self.own = (self.z // 2) == self.core
        self.even = (self.z % 2) == 0
        self.sides = [[2 * i + c for i in range(self.slots)] for c in range(2)]

    def cross(self, values):
        return lax.ppermute(values, ("dp", "mp"), cross_pairs(self.n_dp))

    def side(self, values):
        return lax.ppermute(values, ("dp", "mp"), side_pairs(self.n_dp))

    def ordered(self, mine, other):
        return jnp.where(self.core == 0, jnp.concatenate([mine, other], 0), jnp.concatenate([other, mine], 0))

    def slice_of(self, weight):
        rows = weight.shape[0] // self.slots
        return lax.dynamic_slice_in_dim(weight, self.slot * rows, rows, 0)

    def quarters(self, part, got):
        far = self.side(got)
        first = jnp.where(self.own, part, got)
        second = jnp.where(self.own, got, far)
        return jnp.where(self.even, first, second), jnp.where(self.even, second, first)

    def gathered(self, part):
        return lax.all_gather(part, "dp", axis=0, tiled=True, axis_index_groups=self.sides)

    def gathered_direct(self, part):
        every = jnp.concatenate([part] * self.slots, 0)
        return lax.all_to_all(every, "dp", 0, 0, tiled=True, axis_index_groups=self.sides)

    def gathered_steps(self, part):
        if self.slots != 4:
            return self.gathered(part)
        rows = part.shape[0]
        every = jnp.zeros((4 * rows, part.shape[1]), part.dtype)
        for k, piece in enumerate((part, moved(part, 2), moved(part, 4), moved(part, 6))):
            every = lax.dynamic_update_slice_in_dim(every, piece, (self.slot ^ k) * rows, 0)
        return every

    def gathered_pairs(self, part):
        return lax.all_to_all(jnp.concatenate([part] * self.n_dp, 0), "dp", 0, 0, tiled=True)

    def scattered(self, values):
        return lax.psum_scatter(values, "dp", scatter_dimension=0, tiled=True, axis_index_groups=self.sides)

    def pieces(self, values):
        if self.slots != 4:
            return [self.scattered(values)]
        rows = values.shape[0] // 4
        pick = lambda k: lax.dynamic_slice_in_dim(values, (self.slot ^ k) * rows, rows, 0)
        return [pick(0), moved(pick(1), 2), moved(pick(2), 4), moved(pick(3), 6)]

    def added(self, parts):
        return sum(p.astype(jnp.float32) for p in parts).astype(jnp.bfloat16)

    def swapped(self, values):
        every = lax.all_to_all(values, "dp", 0, 0, tiled=True, axis_index_groups=self.sides)
        return list(every.reshape((self.slots, -1) + every.shape[1:]))

    def bring(self, low, high):
        first = jnp.where(self.even, low, high)
        second = jnp.where(self.even, high, low)
        return first, second, self.side(second)

    def bring_across(self, first, second, far):
        total = (first.astype(jnp.float32) + far.astype(jnp.float32)).astype(jnp.bfloat16)
        return self.cross(jnp.where(self.own, second, total))

    def bring_home(self, first, got):
        f32, bf16 = jnp.float32, jnp.bfloat16
        part = jnp.where(self.own, (first.astype(f32) + got.astype(f32)).astype(bf16), got)
        half = first.shape[0] // 2
        cut = lambda which: lax.dynamic_slice_in_dim(part, which * half, half, 0)
        return (cut(self.core).astype(f32) + moved(cut(1 - self.core), 1).astype(f32)).astype(bf16)


def exchanged(values):
    return lax.all_to_all(values, "mp", 0, 0, tiled=True)


def rms_parts(values):
    inverse = lax.rsqrt(jnp.mean(values * values, axis=-1, keepdims=True) + norm_eps)
    return (values * inverse, inverse)


def rms_back(grad_rows, normed, inverse, gain_vec):
    grad_normed = grad_rows * gain_vec
    return inverse * (grad_normed - normed * jnp.mean(grad_normed * normed, axis=-1, keepdims=True))


def mm(a, b):
    return dot(a, b, 1, 0)


def mm_t(a, b):
    return dot(a, b, 1, 1)


def t_mm(a, b):
    return dot(a, b, 0, 0)


def shards(
    hidden_in,
    first_in,
    segment_ids,
    valid_tokens,
    w_query,
    w_key,
    w_value,
    w_first_value,
    w_out,
    w_gate,
    w_up,
    w_down,
    gain_attn,
    gain_mlp,
    out_cotangent,
):
    at = Place()
    bf16, f32 = jnp.bfloat16, jnp.float32
    rows, width = hidden_in.shape
    cols = w_query.shape[1]
    pairs = cols // 128
    hid = w_gate.shape[1]
    pad = -(-hid // 256) * 256
    beside = lambda *parts: jnp.concatenate(parts, 1)

    slot = at.slot.reshape(1).astype(jnp.int32)
    parts = inner_slices(slot, (w_query, w_key, w_value, w_first_value), at.slots)
    down_rows, out_rows = hid // at.slots, cols // at.slots
    tall = width // at.slots
    got_pair = []
    before = ()
    for part in parts:
        part = tied(part, before)
        before = at.cross(part)
        got_pair.append((part, before))
    wider = jnp.zeros((tall, pad - hid), bf16)
    outer = jnp.concatenate(
        [at.slice_of(w_down), at.slice_of(w_out), jnp.zeros((tall - down_rows - out_rows, width), bf16)], 0
    )
    part = tied(beside(at.slice_of(w_gate), wider, at.slice_of(w_up), wider, outer), before)
    got_feed = (part, at.cross(part))
    near = [beside(*at.quarters(part, got)) for part, got in got_pair]
    w_pair = [at.gathered_direct(tied(near[0], ()))]

    x_all = at.ordered(*tied((hidden_in, moved(hidden_in, 1)), near[0]))
    first_all = at.ordered(*tied((first_in, moved(first_in, 1)), near[0]))
    facts = jnp.stack([segment_ids, valid_tokens])
    facts = tied(at.ordered(facts[None], moved(facts, 1)[None]), near[0])
    seq_places = jax.vmap(token_places)(facts[:, 0])
    live = lax.dynamic_slice_in_dim(facts[:, 1], at.z * rows, rows, 1).reshape(-1, 1).astype(bf16)
    places = lax.dynamic_slice_in_dim(seq_places, at.z * rows, rows, 1).reshape(-1)
    spots = jnp.arange(segment_ids.shape[0], dtype=jnp.int32)
    unit = at.z // 2
    unit_places = lax.dynamic_index_in_dim(seq_places, unit, 0, keepdims=False)
    unit_live = lax.dynamic_index_in_dim(facts[:, 1], unit, 0, keepdims=False)
    first_key = jnp.where(unit_live == 1, spots - unit_places, spots)[None]
    frequency = jnp.exp(jnp.arange(HD // 2, dtype=f32) * (-2.0 * math.log(10000.0) / HD))
    angles = jnp.concatenate([places, unit_places]).astype(f32)[None, :] * frequency[:, None]
    cos_flat, sin_flat = jnp.cos(angles), jnp.sin(angles)
    n_here = 2 * rows
    cosine = jnp.concatenate([cos_flat] * 4, 0).T
    sine = jnp.concatenate([-sin_flat, sin_flat] * 2, 0).T
    flat = jnp.stack([cos_flat[:, n_here:], sin_flat[:, n_here:]])

    normed_one, inverse_one = rms_parts(x_all.astype(f32))
    h_one = (normed_one * gain_attn).astype(bf16)
    kept = []
    mixed = []
    powers = 0.0
    sends = []
    for p in range(pairs):
        if p == 1:
            part, got = got_feed
            feed_part = tied(beside(*at.quarters(part, got)), (sends, first_key, flat, cosine, sine))
        if p:
            w_pair.append(at.gathered_steps(tied(near[p], feed_part)))
        sent, power = project(h_one, first_all, w_pair[p], cosine[:n_here], sine[:n_here])
        powers = powers + jnp.sum(power, 1)
        sends.append(sent)
    full = at.gathered(feed_part)
    span = 2 * pad + width
    both_do = full.reshape(at.slots, tall, 2 * span)
    lanes = lambda q: slice(q * span + 2 * pad, (q + 1) * span)
    nothing = jnp.zeros((pad - hid, width), bf16)
    full_d = jnp.concatenate(
        [a for q in range(2) for a in (both_do[:, :down_rows, lanes(q)].reshape(hid, width), nothing)], 0
    )
    full_o = jnp.concatenate(
        [both_do[:, down_rows : down_rows + out_rows, lanes(q)].reshape(cols, width) for q in range(2)], 0
    )

    for p in range(pairs):
        qkv = exchanged(sends[p])
        attended, logsum = attend(first_key, qkv)
        kept.append((qkv, attended, logsum))
        mixed.append(exchanged(attended))
    dy_own = tied(lax.dynamic_slice_in_dim(out_cotangent, at.z * rows, rows, 0), sends)
    dy_all = at.ordered(dy_own, moved(dy_own, 1))

    own_rows = lambda a: lax.dynamic_slice_in_dim(a, at.core * rows, rows, 0)
    other_rows = lambda a: lax.dynamic_slice_in_dim(a, (1 - at.core) * rows, rows, 0)

    attn_mixed, out_part = mix(mixed, live, full_o)
    residual, h_two, hidden, d_gu, d_part = feed(
        x_all, out_part, moved(out_part, 1), gain_mlp[None], dy_all, full, full_d
    )
    d_other = moved(d_part, 1)
    g_gu = weigh(h_two, d_gu)
    s_gu = at.scattered(g_gu)
    d_res, d_attn, gains, *sends = turn(
        at.core.reshape(1), tied(residual, g_gu), d_part, d_other, dy_all, gain_mlp[None], full_o, live
    )
    incoming = [exchanged(sent) for sent in sends]

    g_down = weigh(tied(hidden, sends), dy_all)
    g_out = weigh(attn_mixed, d_attn)
    blank = jnp.zeros((at.slots, tall - down_rows - out_rows, width), bf16)
    slotted = lambda g, first, n: g[first : first + n].reshape(at.slots, n // at.slots, width)
    g_do = jnp.concatenate(
        [
            jnp.concatenate([slotted(g_down, q * pad, hid), slotted(g_out, q * cols, cols), blank], 1)
            for q in range(2)
        ],
        2,
    ).reshape(-1, 2 * width)
    s_do = at.scattered(g_do)
    backs = []
    key = tied(first_key, (g_down, g_out))
    for p in range(pairs):
        qkv, attended, logsum = kept[p]
        back = attend_back(key, qkv, attended, incoming[p], logsum, flat, cosine[n_here:], sine[n_here:])
        backs.append(exchanged(back))
        if p == 0:
            ffn = multiply(tied(hidden, back), full_d)
            tied_gu = tied(s_gu, back)
            first_gu, second_gu, far_gu = at.bring(tied_gu[:, : 2 * pad], tied_gu[:, 2 * pad :])
            key = tied(key, (far_gu, ffn))
    got_gu = at.bring_across(first_gu, second_gu, far_gu)
    near_gu = at.bring_home(first_gu, got_gu)
    ffn = own_rows(ffn).astype(f32) + moved(other_rows(ffn), 1).astype(f32)
    block_out = (own_rows(residual) + ffn).astype(bf16)

    d_h1 = 0.0
    parts = []
    sent_pair = ()
    for p in range(pairs):
        back = tied(backs[p], (block_out, got_gu, sent_pair))
        d_inner = jnp.concatenate([beside(back[2 * s], back[2 * s + 1]) for s in range(2)], 0)
        d_first = beside(d_inner[:, 256:384], d_inner[:, 640:768])
        w_inner = beside(w_pair[p][:, :384], w_pair[p][:, 512:896])
        d_h1 = d_h1 + mm_t(d_inner, w_inner)
        g_inner = weigh(h_one, d_inner)
        g_first = weigh(first_all, d_first)
        g_pair = beside(g_inner[:, :384], g_first[:, :128], g_inner[:, 384:], g_first[:, 128:])
        parts.append(at.swapped(g_pair) if p else at.pieces(g_pair))
        sent_pair = g_pair
    d_h1 = d_h1.astype(bf16)
    d_h1 = own_rows(d_h1).astype(f32) + moved(other_rows(d_h1), 1).astype(f32)
    own_normed = own_rows(normed_one)
    grad_input = (own_rows(d_res) + rms_back(d_h1, own_normed, own_rows(inverse_one), gain_attn)).astype(bf16)

    gain_parts = jnp.stack([jnp.sum(d_h1 * own_normed, 0), gains[0]])
    small = jnp.concatenate([gain_parts.reshape(-1), powers[:2], jnp.zeros((126,), f32)])
    small = small.reshape(-1, 128)
    small = jnp.pad(small, ((0, -small.shape[0] % 8), (0, 0)))
    for axis, size in (("dp", at.n_dp), ("mp", 4)):
        every = lax.all_to_all(jnp.concatenate([small] * size, 0), axis, 0, 0, tiled=True)
        small = jnp.sum(every.reshape((size,) + small.shape), 0)
    sum_gu = lax.all_gather(near_gu, "dp", axis=0, tiled=True)
    most = at.added(tied(parts[0], backs))
    first, second, far = at.bring(
        *(beside(tied(s_do, back)[:, q * width : (q + 1) * width], most[:, q * 512 : (q + 1) * 512]) for q in range(2))
    )
    got = at.bring_across(first, second, tied(far, (parts, d_h1)))
    late = [at.added(part) for part in parts[1:]]
    late = [at.bring(part[:, :512], part[:, 512:]) for part in late]
    most = at.bring_home(first, tied(got, (late, sum_gu)))
    sum_do = lax.all_gather(most, "dp", axis=0, tiled=True)
    late = [at.bring_home(one, at.bring_across(one, two, tied(three, small))) for one, two, three in late]
    grad_gate, grad_up = spread_gu(sum_gu, pad, hid)
    inner_sums = [(sum_do, width // 512)]
    inner_sums += [(at.gathered_pairs(tied(part, (grad_gate, grad_up))), 0) for part in late]
    if down_rows % 16 == 0:
        grad_down, grad_out = spread_do(sum_do, at.slots, down_rows, out_rows, width)
    else:
        all_do = sum_do[:, :width].reshape(at.slots, tall, width)
        grad_down = all_do[:, :down_rows].reshape(hid, width).astype(f32)
        grad_out = all_do[:, down_rows : down_rows + out_rows].reshape(cols, width).astype(f32)
    small = small.reshape(-1)
    count = float(rows * at.n_dp * 4 * width)
    return (
        block_out,
        grad_input,
        *inner_spread(inner_sums),
        grad_out,
        grad_gate.T,
        grad_up.T,
        grad_down,
        small[:width],
        small[width : 2 * width],
        small[2 * width] / count,
        small[2 * width + 1] / count,
    )


def solution(mesh):
    placed = (
        P(("dp", "mp"), None),
        P(("dp", "mp"), None),
        P("dp"),
        P("dp"),
        P(None, "mp"),
        P(None, "mp"),
        P(None, "mp"),
        P(None, "mp"),
        P("mp", None),
        P(None, "mp"),
        P(None, "mp"),
        P("mp", None),
        P(),
        P(),
        P("dp", None),
    )
    return jax.shard_map(
        shards,
        mesh=mesh,
        in_specs=placed,
        out_specs=(
            P(("dp", "mp"), None),
            P(("dp", "mp"), None),
            P(None, "mp"),
            P(None, "mp"),
            P(None, "mp"),
            P(None, "mp"),
            P("mp", None),
            P(None, "mp"),
            P(None, "mp"),
            P("mp", None),
            P(),
            P(),
            P(),
            P(),
        ),
        check_vma=False,
    )
```
